128 devices in a mesh: dp: 8 (over y, x_lo), ctx: 16 (over x_hi, z, core).
Axes of the slice: x: 4 (x_hi: 2, x_lo: 2; x = x_hi * 2 + x_lo), y: 4, z: 4, core: 2. Of those that a mesh axis runs over, the one named last changes fastest.
Arguments:
- proj: bfloat16 [32768, 3072], P(('dp', 'ctx')), may hold values from -6 to 6
- short_w: float32 [3, 3072], replicated, may hold values from -3.5 to 3.5
- filt: float32 [4096, 1024], P(None, 'ctx'), may hold values from -4 to 4
- skip_gain: float32 [1024], replicated, may hold values from -1 to 1
- cotangent: bfloat16 [32768, 1024], P(('dp', 'ctx')), may hold values from -6 to 6
Outputs:
- outputs: bfloat16 [32768, 1024], P(('dp', 'ctx'))
- proj_grad: bfloat16 [32768, 3072], P(('dp', 'ctx'))
- short_grad: float32 [3, 3072], replicated
- skip_grad: float32 [1024], replicated
- filt_grad: float32 [4096, 1024], P('dp', 'ctx')
The draws below stay inside these ranges and needn't reach their ends.
All inputs are finite; a program needn't handle non-finite values.
Results may differ from the reference program's by a relative error of at most 0.017.
Values may be sent and summed in bfloat16 or wider, within the bound.
A program may use at most 128 MiB of HBM per device.

```python
import math
import jax
import jax.numpy as jnp
from jax import lax

C = 1024
SHORT = 3
LEN = 4096
TOKENS = 32768


def draw_filt(key, part):
    key = jax.random.fold_in(key, 7)
    rate_key, noise_key = jax.random.split(key)
    offsets = jnp.arange(LEN, dtype=jnp.float32)[:, None]
    log_rate = jax.random.uniform(rate_key, (1, C), jnp.float32, math.log(1.0 / LEN), math.log(1.0 / 32.0))
    noise = jnp.clip(jax.random.normal(noise_key, (LEN, C), jnp.float32), -4.0, 4.0)
    decay_rate = jnp.exp(log_rate)
    norming = jnp.sqrt((1.0 - jnp.exp(-2.0 * decay_rate)) / (1.0 - jnp.exp(-2.0 * decay_rate * LEN)))
    return (noise * jnp.exp(-decay_rate * offsets) * norming).astype(jnp.float32)


def block_levels(rng, shape, cuts, smallest, high):
    def one(axis_at, blocks):
        heights = jax.random.uniform(jax.random.fold_in(jax.random.fold_in(rng, 6), axis_at), (blocks,), jnp.float32, smallest / len(cuts), high / len(cuts))
        return jnp.repeat(jnp.exp(heights), shape[axis_at] // blocks).reshape((-1,) + (1,) * (len(shape) - axis_at - 1))

    factor_of = one(*cuts[0])
    for cut in cuts[1:]:
        factor_of = factor_of * one(*cut)
    return factor_of


def scatter_about(own_key, extent, scale, reach, cuts=(), held_as=jnp.bfloat16):
    drawn = jax.random.normal(own_key, extent, jnp.float32) * scale
    if len(cuts) > 0:
        drawn = block_levels(own_key, extent, cuts, -0.22, 0.18) * drawn
    return jnp.clip(drawn, min=-reach, max=reach).astype(held_as)


def setup_inputs(seed: int = 0) -> dict:
    keys = jax.random.split(jax.random.key(seed), 6)
    return {
        "proj": scatter_about(keys[0], (TOKENS, 3 * C), 1.0, 6.0, ((0, 128),)),
        "short_w": scatter_about(keys[1], (SHORT, 3 * C), SHORT ** -0.5, 3.5, (), jnp.float32),
        "filt": draw_filt(jax.random.fold_in(keys[5], 71), 0),
        "skip_gain": jnp.clip(jax.random.uniform(keys[3], (C,), jnp.float32, -1.0, 1.0), -1.0, 1.0),
        "cotangent": scatter_about(keys[4], (TOKENS, C), 1.0, 6.0, ((0, 128),)),
    }


def spectrum(signal):
    return jnp.fft.rfft(signal, n=2 * LEN, axis=0)

def back_to_time(freq):
    return jnp.fft.irfft(freq, n=2 * LEN, axis=0)[:LEN]

def rounded(values):
    return lax.optimization_barrier(values.astype(jnp.bfloat16)).astype(jnp.float32)

def reference(proj, short_w, filt, skip_gain, cotangent):
    width = skip_gain.shape[0]
    taps = short_w.shape[0]
    filt_freq = spectrum(filt)
    out_list = []
    grad_list = []
    short_total = jnp.zeros(short_w.shape, jnp.float32)
    skip_total = jnp.zeros((width,), jnp.float32)
    filt_total = jnp.zeros(filt.shape, jnp.float32)
    for seq_index in range(TOKENS // LEN):
        rows = proj[seq_index * LEN:(seq_index + 1) * LEN].astype(jnp.float32)
        padded = jnp.pad(rows, ((taps - 1, 0), (0, 0)))
        mixed = jnp.zeros(rows.shape, jnp.float32)
        for lag in range(taps):
            mixed = mixed + short_w[lag] * padded[taps - 1 - lag:taps - 1 - lag + LEN]
        queries = mixed[:, :width]
        keys_part = mixed[:, width:2 * width]
        values_part = mixed[:, 2 * width:]
        product = rounded(keys_part * values_part)
        long_part = rounded(back_to_time(spectrum(product) * filt_freq))
        gated_in = long_part + skip_gain * product
        out_list.append((queries * gated_in).astype(jnp.bfloat16))
        cot_rows = cotangent[seq_index * LEN:(seq_index + 1) * LEN].astype(jnp.float32)
        conv_grad = rounded(cot_rows * queries)
        grad_freq = spectrum(conv_grad)
        back_part = rounded(back_to_time(grad_freq * jnp.conj(filt_freq)))
        product_grad = back_part + skip_gain * conv_grad
        mixed_grad = rounded(jnp.concatenate([cot_rows * gated_in, product_grad * values_part, product_grad * keys_part], axis=1))
        padded_grad = jnp.pad(mixed_grad, ((0, taps - 1), (0, 0)))
        proj_rows = jnp.zeros(rows.shape, jnp.float32)
        for lag in range(taps):
            proj_rows = proj_rows + short_w[lag] * padded_grad[lag:lag + LEN]
        grad_list.append(proj_rows.astype(jnp.bfloat16))
        short_total = short_total + jnp.stack([lax.optimization_barrier(jnp.sum(mixed_grad * padded[taps - 1 - lag:taps - 1 - lag + LEN], axis=0)) for lag in range(taps)])
        skip_total = skip_total + lax.optimization_barrier(jnp.sum(conv_grad * product, axis=0))
        filt_total = filt_total + back_to_time(grad_freq * jnp.conj(spectrum(product)))
    scale = 1.0 / math.sqrt(TOKENS)
    return (jnp.concatenate(out_list, axis=0), jnp.concatenate(grad_list, axis=0), short_total * scale, skip_total * scale, filt_total * scale)
```

```python
import functools
import math

import jax
import jax.numpy as jnp
import ml_dtypes
import numpy as np
from jax import lax
from jax.experimental import pallas as pl
from jax.experimental.pallas import tpu as pltpu
from jax.sharding import PartitionSpec as P

HI = 256
LO = 16
GROUP = 8
GROUPS = HI // GROUP
LANES = 128
HALF = 64
MESH = pl.DeviceIdType.MESH
F32 = jnp.float32
BF16 = jnp.bfloat16


def tables():
    total = HI * LO
    start = np.arange(HI)
    angle = 2.0 * math.pi / HI * ((start[:, None] + 0.25) * np.arange(HI)[None, :] % HI)
    first = np.stack([np.cos(angle), -np.sin(angle)])
    first = first.reshape(2, GROUPS, GROUP, HI).transpose(1, 0, 2, 3).reshape(2 * HI, HI)
    freq = HI * np.arange(LO)[None, None, :] + start.reshape(GROUPS, GROUP)[:, :, None] + 0.25
    angle = 2.0 * math.pi / total * (freq[..., None] * np.arange(LO) % total)
    second = np.zeros((GROUPS, 2, LO, GROUP, LO, 2, GROUP))
    for at in range(GROUP):
        second[:, 0, :, at, :, 0, at] = np.cos(angle[:, at])
        second[:, 0, :, at, :, 1, at] = np.sin(angle[:, at])
        second[:, 1, :, at, :, 0, at] = -np.sin(angle[:, at])
        second[:, 1, :, at, :, 1, at] = np.cos(angle[:, at])
    second = second.reshape(GROUPS, 2 * LO * GROUP, 2 * LO * GROUP)
    rows = np.arange(256)
    perm = np.zeros((256, 256))
    perm[rows, rows % 16 * LO + rows // 16] = 1.0
    return [
        table.astype(ml_dtypes.bfloat16)
        for table in (perm, perm.T, first, second, first.T / total, second.transpose(0, 2, 1))
    ]


def dot(left, right):
    return jnp.dot(left, right, preferred_element_type=F32)


def low_lanes(rows):
    return lax.broadcasted_iota(jnp.int32, (rows, LANES), 1) < HALF


def delayed(x, rim, steps):
    turned = pltpu.roll(x, steps, 0)
    before = pltpu.roll(rim, steps, 0)
    row = lax.broadcasted_iota(jnp.int32, (8, LANES), 0)
    return jnp.concatenate([jnp.where(row < steps, before, turned[:8]), turned[8:]], axis=0)


def advanced(x, steps):
    rows = x.shape[0]
    turned = pltpu.roll(x, rows - steps, 0)
    row = lax.broadcasted_iota(jnp.int32, (8, LANES), 0)
    return jnp.concatenate(
        [turned[: rows - 8], jnp.where(row < 8 - steps, turned[rows - 8 :], 0.0)], axis=0
    )


def kernel(
    scale,
    proj_h, cot_h, filt_h, short_h, skip_h, perm_h, unperm_h, first_h, second_h, firstt_h, secondt_h,
    out_h, pg_h, sg_h, skg_h, fg_h,
    proj_v, cot_v, filt_v, short_v, skip_v, perm_v, unperm_v, first_v, second_v, firstt_v, secondt_v,
    rim_v, mix_v, send_v, recv_v, fx_v, y_v, fs_v, z_v, ysend_v, brecv_v, fsend_v, frecv_v,
    out_v, pg_v, tail_v, rsend_v, rrecv_v, asend_v, arecv_v, dsend_v, drecv_v, gsend_v, grecv_v,
    sg_v, skg_v, fg_v,
    load_sem, rim_ss, rim_rs, a_ss, a_rs, b_ss, b_rs, f_ss, f_rs, r_ss, r_rs, s_ss, s_rs, d_ss, d_rs,
    g_ss, g_rs, local_sem, store_sem,
):
    me = lax.axis_index("ctx")
    dpi = lax.axis_index("dp")
    chip = me // 2
    nxt = lax.rem(me + 1, 16)
    prv = lax.rem(me + 15, 16)

    barrier = pltpu.get_barrier_semaphore()
    for step in range(1, 16):
        pl.semaphore_signal(
            barrier, inc=1, device_id={"ctx": lax.rem(me + step, 16)}, device_id_type=MESH
        )
    for step in range(1, 8):
        pl.semaphore_signal(
            barrier, inc=1, device_id={"dp": lax.rem(dpi + step, 8)}, device_id_type=MESH
        )

    loads = [
        pltpu.make_async_copy(src, dst, load_sem.at[at])
        for at, (src, dst) in enumerate(
            [
                (proj_h, proj_v), (cot_h, cot_v), (short_h, short_v), (perm_h, perm_v), (filt_h, filt_v),
                (first_h, first_v), (second_h, second_v), (secondt_h, secondt_v), (firstt_h, firstt_v),
                (unperm_h, unperm_v), (skip_h, skip_v),
            ]
        )
    ]
    for load in loads:
        load.start()
    asend_v[...] = jnp.zeros_like(asend_v)
    pl.semaphore_wait(barrier, 22)

    def rim_copy(to):
        return pltpu.make_async_remote_copy(
            src_ref=proj_h.at[pl.ds(240, 16), :], dst_ref=rim_v, send_sem=rim_ss.at[0], recv_sem=rim_rs.at[0],
            device_id={"ctx": to}, device_id_type=MESH,
        )

    rim_copy(nxt).start()
    for load in loads[:4]:
        load.wait()
    rim_copy(nxt).wait()
    keep = jnp.where(me == 0, 0.0, 1.0).astype(F32)

    def forward_copy(to, source):
        return pltpu.make_async_remote_copy(
            src_ref=send_v.at[to], dst_ref=recv_v.at[:, pl.ds(pl.multiple_of(source * 16, 16), 16), :],
            send_sem=a_ss.at[to], recv_sem=a_rs.at[source], device_id={"ctx": to}, device_id_type=MESH,
        )

    def gate_tile(step, carry):
        tile = lax.rem(chip + step, 8)
        cols = pl.ds(pl.multiple_of(tile * LANES, LANES), LANES)
        mixed = []
        for part in range(3):
            cut = pl.ds(pl.multiple_of(tile * LANES + part * 1024, LANES), LANES)
            x = proj_v[:, cut].astype(F32)
            rim = rim_v[:, cut].astype(F32)[8:16] * keep
            w = short_v[:, cut]
            value = w[0:1] * x + w[1:2] * delayed(x, rim, 1) + w[2:3] * delayed(x, rim, 2)
            mix_v[part, :, cols] = value
            mixed.append(value)
        product = (mixed[1] * mixed[2]).astype(BF16)
        grad = (cot_v[:, cols].astype(F32) * mixed[0]).astype(BF16)
        both = dot(perm_v[...], jnp.concatenate([product, grad], axis=1))
        p, g = both[:, :LANES], both[:, LANES:]
        low = low_lanes(256)
        even = jnp.where(low, p, pltpu.roll(g, HALF, 1))
        odd = jnp.where(low, pltpu.roll(p, HALF, 1), g)
        send_v[2 * tile] = even.astype(BF16).reshape(16, 16, LANES)
        send_v[2 * tile + 1] = odd.astype(BF16).reshape(16, 16, LANES)
        for core in range(2):

            @pl.when(2 * tile + core != me)
            def _():
                forward_copy(2 * tile + core, me).start()

        return carry

    lax.fori_loop(1, 9, gate_tile, 0)
    own = pltpu.make_async_copy(
        send_v.at[me], recv_v.at[:, pl.ds(pl.multiple_of(me * 16, 16), 16), :], local_sem.at[0]
    )
    own.start()

    def first_stage(source, pair, carry):
        x = jnp.concatenate([source[2 * pair], source[2 * pair + 1]], axis=1)
        y = dot(first_v[...], x).astype(BF16)
        y_v[2 * pair] = y[:, :LANES]
        y_v[2 * pair + 1] = y[:, LANES:]
        return carry

    def second_stage(group):
        rows = y_v[:, pl.ds(pl.multiple_of(group * 16, 16), 16), :].reshape(256, LANES)
        return dot(second_v[group], rows)

    for load in loads[4:7]:
        load.wait()

    def filter_rows(block, carry):
        x = filt_v[pl.ds(pl.multiple_of(block * 256, 256), 256), :]
        x = jnp.concatenate([x, x], axis=1).astype(BF16)
        x = dot(perm_v[...], x).astype(BF16).reshape(16, 16, LANES)
        fx_v[:, pl.ds(pl.multiple_of(block * 16, 16), 16), :] = x
        return carry

    def filter_group(group, carry):
        spec = second_stage(group)
        fs_v[group, :LANES] = spec[:LANES]
        fs_v[group, LANES:] = jnp.where(low_lanes(LANES), spec[LANES:], -spec[LANES:])
        return carry

    lax.fori_loop(0, 16, filter_rows, 0)
    lax.fori_loop(0, 8, functools.partial(first_stage, fx_v), 0)
    lax.fori_loop(0, GROUPS, filter_group, 0)
    for load in loads[7:]:
        load.wait()

    own.wait()

    def wait_forward(step, carry):
        forward_copy(me, lax.rem(me + step, 16)).wait_recv()
        return carry

    lax.fori_loop(1, 16, wait_forward, 0)

    lax.fori_loop(0, 8, functools.partial(first_stage, recv_v), 0)

    def middle_group(group, carry):
        spec = second_stage(group)
        sr, si = spec[:LANES], spec[LANES:]
        fr, fi = fs_v[group, :LANES], fs_v[group, LANES:]
        rr, ri = pltpu.roll(sr, HALF, 1), pltpu.roll(si, HALF, 1)
        cross = ri * sr - rr * si
        low = low_lanes(LANES)
        real = jnp.concatenate([sr * fr - si * fi, sr * rr + si * ri], axis=1)
        imag = jnp.concatenate([sr * fi + si * fr, jnp.where(low, cross, -cross)], axis=1)
        freq = jnp.concatenate([real, imag], axis=0).astype(BF16)
        back = dot(secondt_v[group], freq).astype(BF16).reshape(16, 16, 2 * LANES)
        z_v[:, pl.ds(pl.multiple_of(group * 16, 16), 16), :] = back
        return carry

    lax.fori_loop(0, GROUPS, middle_group, 0)

    def last_stage(pair, carry):
        even = dot(firstt_v[...], z_v[2 * pair])
        odd = dot(firstt_v[...], z_v[2 * pair + 1])
        ysend_v[2 * pair] = even[:, :LANES].astype(BF16)
        ysend_v[2 * pair + 1] = odd[:, :LANES].astype(BF16)
        grad = jnp.where(low_lanes(256), even[:, LANES:], odd[:, LANES:]) * scale
        fsend_v[pair] = grad.astype(BF16)
        return carry

    def back_copy(to, source, half):
        return pltpu.make_async_remote_copy(
            src_ref=ysend_v.at[pl.ds(half * 8, 8), pl.ds(pl.multiple_of(to * 16, 16), 16), :],
            dst_ref=brecv_v.at[source, pl.ds(half * 8, 8)],
            send_sem=b_ss.at[half, to], recv_sem=b_rs.at[half, source],
            device_id={"ctx": to}, device_id_type=MESH,
        )

    for half in range(2):
        lax.fori_loop(4 * half, 4 * half + 4, last_stage, 0)

        def send_back(step, carry, half=half):
            back_copy(lax.rem(me + step, 16), me, half).start()
            return carry

        lax.fori_loop(1, 16, send_back, 0)

    def filter_copy(to, source):
        return pltpu.make_async_remote_copy(
            src_ref=fsend_v.at[:, pl.ds(pl.multiple_of(to * 32, 32), 32), :], dst_ref=frecv_v.at[source],
            send_sem=f_ss.at[to], recv_sem=f_rs.at[source], device_id={"dp": to}, device_id_type=MESH,
        )

    def send_filter(step, carry):
        filter_copy(lax.rem(dpi + step, 8), dpi).start()
        return carry

    lax.fori_loop(1, 8, send_filter, 0)
    own_back = pltpu.make_async_copy(
        ysend_v.at[:, pl.ds(pl.multiple_of(me * 16, 16), 16), :], brecv_v.at[me], local_sem.at[1]
    )
    own_back.start()
    own_filter = pltpu.make_async_copy(
        fsend_v.at[:, pl.ds(pl.multiple_of(dpi * 32, 32), 32), :], frecv_v.at[dpi], local_sem.at[2]
    )
    own_filter.start()
    own_back.wait()
    own_filter.wait()

    def rim_back_copy(tile, to):
        return pltpu.make_async_remote_copy(
            src_ref=rsend_v.at[tile], dst_ref=rrecv_v.at[tile], send_sem=r_ss.at[tile], recv_sem=r_rs.at[tile],
            device_id={"ctx": to}, device_id_type=MESH,
        )

    def sum_copy(to, source):
        return pltpu.make_async_remote_copy(
            src_ref=asend_v.at[to], dst_ref=arecv_v.at[source], send_sem=s_ss.at[to], recv_sem=s_rs.at[source],
            device_id={"ctx": to}, device_id_type=MESH,
        )

    def down(x):
        return jnp.sum(x, axis=0, keepdims=True)

    def grad_tile(step, carry):
        tile = lax.rem(chip + step, 8)
        cols = pl.ds(pl.multiple_of(tile * LANES, LANES), LANES)
        for core in range(2):

            @pl.when(2 * tile + core != me)
            def _():
                back_copy(me, 2 * tile + core, 0).wait_recv()
                back_copy(me, 2 * tile + core, 1).wait_recv()

        pair = jnp.concatenate(
            [brecv_v[2 * tile].reshape(256, LANES), brecv_v[2 * tile + 1].reshape(256, LANES)], axis=1
        )
        pair = dot(unperm_v[...], pair)
        even, odd = pair[:, :LANES], pair[:, LANES:]
        low = low_lanes(256)
        long_part = jnp.where(low, even, pltpu.roll(odd, HALF, 1))
        back_part = jnp.where(low, pltpu.roll(even, HALF, 1), odd)
        queries, keys, values = (mix_v[part, :, cols] for part in range(3))
        cot = cot_v[:, cols].astype(F32)
        gain = skip_v[:, cols]
        product = (keys * values).astype(BF16).astype(F32)
        grad = (cot * queries).astype(BF16).astype(F32)
        gated = long_part + gain * product
        out_v[:, cols] = (queries * gated).astype(BF16)
        product_grad = back_part + gain * grad
        for part, mixed_grad in enumerate((cot * gated, product_grad * values, product_grad * keys)):
            cut = pl.ds(pl.multiple_of(tile * LANES + part * 1024, LANES), LANES)
            rounded = mixed_grad.astype(BF16)
            rsend_v[tile, 16 * part : 16 * part + 16] = rounded[:16]
            mg = rounded.astype(F32)
            one, two = advanced(mg, 1), advanced(mg, 2)
            w = short_v[:, cut]
            value = w[0:1] * mg + w[1:2] * one + w[2:3] * two
            pg_v[:, cut] = value.astype(BF16)
            tail_v[tile, 16 * part : 16 * part + 16] = value[240:]
            x = proj_v[:, cut].astype(F32)
            rim = rim_v[:, cut].astype(F32)[8:16] * keep
            head = mg[:8]
            sums = [
                down(mg * x),
                down(one * x) + head[0:1] * rim[7:8],
                down(two * x) + head[0:1] * rim[6:7] + head[1:2] * rim[7:8],
            ]
            for tap in range(3):
                at = 3 * part + tap
                asend_v[2 * tile + at // 8, at % 8 : at % 8 + 1] = sums[tap]
        asend_v[2 * tile + 1, 1:2] = down(grad * product)
        rim_back_copy(tile, prv).start()
        for core in range(2):

            @pl.when(2 * tile + core != me)
            def _():
                sum_copy(2 * tile + core, me).start()

        return carry

    lax.fori_loop(1, 9, grad_tile, 0)
    arecv_v[me] = asend_v[me]
    stores = [
        pltpu.make_async_copy(out_v, out_h, store_sem.at[0]),
        pltpu.make_async_copy(pg_v.at[pl.ds(0, 240)], pg_h.at[pl.ds(0, 240)], store_sem.at[1]),
    ]
    for store in stores:
        store.start()

    def wait_sums(step, carry):
        sum_copy(me, lax.rem(me + step, 16)).wait_recv()
        return carry

    lax.fori_loop(1, 16, wait_sums, 0)
    total = arecv_v[0]
    for at in range(1, 16):
        total = total + arecv_v[at]
    dsend_v[...] = total
    drecv_v[dpi] = total

    def part_copy(to, source):
        return pltpu.make_async_remote_copy(
            src_ref=dsend_v, dst_ref=drecv_v.at[source], send_sem=d_ss.at[to], recv_sem=d_rs.at[source],
            device_id={"dp": to}, device_id_type=MESH,
        )

    def all_copy(to, source):
        return pltpu.make_async_remote_copy(
            src_ref=gsend_v, dst_ref=grecv_v.at[source], send_sem=g_ss.at[to], recv_sem=g_rs.at[source],
            device_id={"ctx": to}, device_id_type=MESH,
        )

    def send_part(step, carry):
        part_copy(lax.rem(dpi + step, 8), dpi).start()
        return carry

    lax.fori_loop(1, 8, send_part, 0)

    def wait_filter(step, carry):
        filter_copy(dpi, lax.rem(dpi + step, 8)).wait_recv()
        return carry

    lax.fori_loop(1, 8, wait_filter, 0)
    for pair in range(8):
        value = frecv_v[0, pair].astype(F32)
        for at in range(1, 8):
            value = value + frecv_v[at, pair].astype(F32)
        fg_v[pl.ds(2 * pair, 32, 16), :] = value[:, :HALF]
        fg_v[pl.ds(2 * pair + 1, 32, 16), :] = pltpu.roll(value, HALF, 1)[:, :HALF]
    store = pltpu.make_async_copy(fg_v, fg_h, store_sem.at[2])
    store.start()
    stores.append(store)

    def wait_part(step, carry):
        part_copy(dpi, lax.rem(dpi + step, 8)).wait_recv()
        return carry

    lax.fori_loop(1, 8, wait_part, 0)
    total = drecv_v[0]
    for at in range(1, 8):
        total = total + drecv_v[at]
    total = total * scale
    gsend_v[...] = total
    grecv_v[me] = total

    def send_all(step, carry):
        all_copy(lax.rem(me + step, 16), me).start()
        return carry

    lax.fori_loop(1, 16, send_all, 0)

    keep_back = jnp.where(me == 15, 0.0, 1.0).astype(F32)

    def fix_tile(tile, carry):
        rim_back_copy(tile, prv).wait_recv()
        row = lax.broadcasted_iota(jnp.int32, (16, LANES), 0)
        for part in range(3):
            cut = pl.ds(pl.multiple_of(tile * LANES + part * 1024, LANES), LANES)
            rim = rrecv_v[tile, 16 * part : 16 * part + 16].astype(F32) * keep_back
            w = short_v[:, cut]
            value = tail_v[tile, 16 * part : 16 * part + 16]
            value = value + jnp.where(row == 15, w[1:2] * rim[0:1] + w[2:3] * rim[1:2], 0.0)
            value = value + jnp.where(row == 14, w[2:3] * rim[0:1], 0.0)
            pg_v[pl.ds(240, 16), cut] = value.astype(BF16)
        return carry

    lax.fori_loop(0, 8, fix_tile, 0)
    store = pltpu.make_async_copy(pg_v.at[pl.ds(240, 16)], pg_h.at[pl.ds(240, 16)], store_sem.at[3])
    store.start()
    stores.append(store)

    def wait_all(step, carry):
        all_copy(me, lax.rem(me + step, 16)).wait_recv()
        return carry

    lax.fori_loop(1, 16, wait_all, 0)
    for tile in range(8):
        for at in range(9):
            part, tap = at // 3, at % 3
            left = part * 1024 + tile * LANES
            sg_v[tap : tap + 1, left : left + LANES] = grecv_v[2 * tile + at // 8, at % 8 : at % 8 + 1]
        skg_v[:, tile * LANES : tile * LANES + LANES] = grecv_v[2 * tile + 1, 1:2]
    for at, (src, dst) in enumerate([(sg_v, sg_h), (skg_v, skg_h)]):
        store = pltpu.make_async_copy(src, dst, store_sem.at[4 + at])
        store.start()
        stores.append(store)

    def wait_sends(step, carry):
        to = lax.rem(me + step, 16)
        forward_copy(to, me).wait_send()
        back_copy(to, me, 0).wait_send()
        back_copy(to, me, 1).wait_send()
        sum_copy(to, me).wait_send()
        all_copy(to, me).wait_send()
        return carry

    def wait_dp_sends(step, carry):
        to = lax.rem(dpi + step, 8)
        filter_copy(to, dpi).wait_send()
        part_copy(to, dpi).wait_send()
        return carry

    def wait_rim_sends(tile, carry):
        rim_back_copy(tile, prv).wait_send()
        return carry

    lax.fori_loop(1, 16, wait_sends, 0)
    lax.fori_loop(1, 8, wait_dp_sends, 0)
    lax.fori_loop(0, 8, wait_rim_sends, 0)
    for store in stores:
        store.wait()


def shards(proj, short_w, filt, skip_gain, cotangent):
    width = skip_gain.shape[0]
    scale = 1.0 / math.sqrt(proj.shape[0] * lax.axis_size("dp") * lax.axis_size("ctx"))
    whole = pl.BlockSpec(memory_space=pl.ANY)
    dma = pltpu.SemaphoreType.DMA
    outs = pl.pallas_call(
        functools.partial(kernel, scale),
        out_shape=[
            jax.ShapeDtypeStruct((256, 1024), BF16),
            jax.ShapeDtypeStruct((256, 3072), BF16),
            jax.ShapeDtypeStruct((3, 3072), F32),
            jax.ShapeDtypeStruct((1, 1024), F32),
            jax.ShapeDtypeStruct((512, HALF), F32),
        ],
        in_specs=[whole] * 11,
        out_specs=[whole] * 5,
        scratch_shapes=[
            pltpu.VMEM((256, 3072), BF16),
            pltpu.VMEM((256, 1024), BF16),
            pltpu.VMEM((4096, HALF), F32),
            pltpu.VMEM((3, 3072), F32),
            pltpu.VMEM((1, 1024), F32),
            pltpu.VMEM((256, 256), BF16),
            pltpu.VMEM((256, 256), BF16),
            pltpu.VMEM((2 * HI, HI), BF16),
            pltpu.VMEM((GROUPS, 256, 256), BF16),
            pltpu.VMEM((HI, 2 * HI), BF16),
            pltpu.VMEM((GROUPS, 256, 256), BF16),
            pltpu.VMEM((16, 3072), BF16),
            pltpu.VMEM((3, 256, 1024), F32),
            pltpu.VMEM((16, 16, 16, LANES), BF16),
            pltpu.VMEM((LO, HI, LANES), BF16),
            pltpu.VMEM((LO, HI, LANES), BF16),
            pltpu.VMEM((LO, 2 * HI, LANES), BF16),
            pltpu.VMEM((GROUPS, 256, LANES), F32),
            pltpu.VMEM((LO, 2 * HI, 2 * LANES), BF16),
            pltpu.VMEM((LO, HI, LANES), BF16),
            pltpu.VMEM((16, LO, 16, LANES), BF16),
            pltpu.VMEM((8, HI, LANES), BF16),
            pltpu.VMEM((8, 8, 32, LANES), BF16),
            pltpu.VMEM((256, 1024), BF16),
            pltpu.VMEM((256, 3072), BF16),
            pltpu.VMEM((8, 48, LANES), F32),
            pltpu.VMEM((8, 48, LANES), BF16),
            pltpu.VMEM((8, 48, LANES), BF16),
            pltpu.VMEM((16, 8, LANES), F32),
            pltpu.VMEM((16, 8, LANES), F32),
            pltpu.VMEM((8, LANES), F32),
            pltpu.VMEM((8, 8, LANES), F32),
            pltpu.VMEM((8, LANES), F32),
            pltpu.VMEM((16, 8, LANES), F32),
            pltpu.VMEM((3, 3072), F32),
            pltpu.VMEM((1, 1024), F32),
            pltpu.VMEM((512, HALF), F32),
            dma((11,)),
            dma((1,)), dma((1,)), dma((16,)), dma((16,)), dma((2, 16)), dma((2, 16)), dma((8,)), dma((8,)),
            dma((8,)), dma((8,)), dma((16,)), dma((16,)), dma((8,)), dma((8,)), dma((16,)), dma((16,)),
            dma((3,)), dma((6,)),
        ],
        compiler_params=pltpu.CompilerParams(
            collective_id=0, has_side_effects=True, vmem_limit_bytes=56 * 1024 * 1024
        ),
    )(proj, cotangent, filt, short_w, skip_gain.reshape(1, width), *tables())
    outputs, proj_grad, short_grad, skip_grad, filt_grad = outs
    return (outputs, proj_grad, short_grad, skip_grad.reshape(width), filt_grad)


def solution(mesh):
    placed = (P(("dp", "ctx"), None), P(), P(None, "ctx"), P(), P(("dp", "ctx"), None))
    return jax.shard_map(
        shards,
        mesh=mesh,
        in_specs=placed,
        out_specs=(P(("dp", "ctx"), None), P(("dp", "ctx"), None), P(), P(), P("dp", "ctx")),
        check_vma=False,
    )
```

```python
import functools
import math

import jax
import jax.numpy as jnp
import ml_dtypes
import numpy as np
from jax import lax
from jax.experimental import pallas as pl
from jax.experimental.pallas import tpu as pltpu
from jax.sharding import PartitionSpec as P

HI = 256
LO = 16
GROUP = 8
GROUPS = HI // GROUP
UNROLL = 4
LANES = 128
HALF = 64
MESH = pl.DeviceIdType.MESH
F32 = jnp.float32
BF16 = jnp.bfloat16


def tables():
    total = HI * LO
    start = np.arange(HI)
    angle = 2.0 * math.pi / HI * ((start[:, None] + 0.25) * np.arange(HI)[None, :] % HI)
    first = np.stack([np.cos(angle), -np.sin(angle)])
    first = first.reshape(2, GROUPS, GROUP, HI).transpose(1, 0, 2, 3).reshape(2 * HI, HI)
    freq = HI * np.arange(LO)[None, None, :] + start.reshape(GROUPS, GROUP)[:, :, None] + 0.25
    angle = 2.0 * math.pi / total * (freq[..., None] * np.arange(LO) % total)
    second = np.zeros((GROUPS, 2, LO, GROUP, LO, 2, GROUP))
    for at in range(GROUP):
        second[:, 0, :, at, :, 0, at] = np.cos(angle[:, at])
        second[:, 0, :, at, :, 1, at] = np.sin(angle[:, at])
        second[:, 1, :, at, :, 0, at] = -np.sin(angle[:, at])
        second[:, 1, :, at, :, 1, at] = np.cos(angle[:, at])
    second = second.reshape(GROUPS, 2 * LO * GROUP, 2 * LO * GROUP)
    rows = np.arange(256)
    perm = np.zeros((256, 256))
    perm[rows, rows % 16 * LO + rows // 16] = 1.0
    return [
        table.astype(ml_dtypes.bfloat16)
        for table in (perm, perm.T, first, second, first.T / total, second.transpose(0, 2, 1))
    ]


def dot(left, right):
    return jnp.dot(left, right, preferred_element_type=F32)


def low_lanes(rows):
    return lax.broadcasted_iota(jnp.int32, (rows, LANES), 1) < HALF


def delayed(x, rim, steps):
    turned = pltpu.roll(x, steps, 0)
    before = pltpu.roll(rim, steps, 0)
    row = lax.broadcasted_iota(jnp.int32, (8, LANES), 0)
    return jnp.concatenate([jnp.where(row < steps, before, turned[:8]), turned[8:]], axis=0)


def advanced(x, steps):
    rows = x.shape[0]
    turned = pltpu.roll(x, rows - steps, 0)
    row = lax.broadcasted_iota(jnp.int32, (8, LANES), 0)
    return jnp.concatenate(
        [turned[: rows - 8], jnp.where(row < 8 - steps, turned[rows - 8 :], 0.0)], axis=0
    )


def kernel(
    scale,
    proj_h, cot_h, filt_h, short_h, skip_h, perm_h, unperm_h, first_h, second_h, firstt_h, secondt_h,
    out_v, pg_v, sg_v, skg_v, fg_v,
    proj_v, cot_v, filt_v, short_v, skip_v, perm_v, unperm_v, first_v, second_v, firstt_v, secondt_v,
    rim_v, mix_v, send_v, recv_v, fx_v, y_v, fs_v, spec_v, z_v, ysend_v, brecv_v, fsend_v, frecv_v, hsend_v, hrecv_v,
    tail_v, rsend_v, rrecv_v, asend_v, arecv_v, dsend_v, drecv_v, gsend_v, grecv_v, wide_v,
    load_sem, rim_ss, rim_rs, a_ss, a_rs, b_ss, b_rs, f_ss, f_rs, h_ss, h_rs, r_ss, r_rs, s_ss, s_rs, d_ss, d_rs,
    g_ss, g_rs, local_sem,
):
    me = lax.axis_index("ctx")
    dpi = lax.axis_index("dp")
    chip = me // 2
    nxt = lax.rem(me + 1, 16)
    prv = lax.rem(me + 15, 16)

    barrier = pltpu.get_barrier_semaphore()
    for step in range(1, 16):
        pl.semaphore_signal(
            barrier, inc=1, device_id={"ctx": lax.rem(me + step, 16)}, device_id_type=MESH
        )
    for step in range(1, 8):
        pl.semaphore_signal(
            barrier, inc=1, device_id={"dp": lax.rem(dpi + step, 8)}, device_id_type=MESH
        )

    loads = [
        pltpu.make_async_copy(src, dst, load_sem.at[at])
        for at, (src, dst) in enumerate(
            [
                (proj_h, proj_v), (cot_h, cot_v), (short_h, short_v), (perm_h, perm_v), (filt_h, filt_v),
                (first_h, first_v), (second_h, second_v), (secondt_h, secondt_v), (firstt_h, firstt_v),
                (unperm_h, unperm_v), (skip_h, skip_v),
            ]
        )
    ]
    for load in loads:
        load.start()
    asend_v[...] = jnp.zeros_like(asend_v)
    pl.semaphore_wait(barrier, 22)

    def rim_copy(to):
        return pltpu.make_async_remote_copy(
            src_ref=proj_h.at[pl.ds(240, 16), :], dst_ref=rim_v, send_sem=rim_ss.at[0], recv_sem=rim_rs.at[0],
            device_id={"ctx": to}, device_id_type=MESH,
        )

    rim_copy(nxt).start()
    for load in loads[:4]:
        load.wait()
    rim_copy(nxt).wait()
    keep = jnp.where(me == 0, 0.0, 1.0).astype(F32)

    def forward_copy(to, source):
        return pltpu.make_async_remote_copy(
            src_ref=send_v.at[to], dst_ref=recv_v.at[:, pl.ds(pl.multiple_of(source * 16, 16), 16), :],
            send_sem=a_ss.at[0], recv_sem=a_rs.at[0], device_id={"ctx": to}, device_id_type=MESH,
        )

    def gate_tile(step, carry):
        tile = lax.rem(chip + step, 8)
        cols = pl.ds(pl.multiple_of(tile * LANES, LANES), LANES)
        mixed = []
        for part in range(3):
            cut = pl.ds(pl.multiple_of(tile * LANES + part * 1024, LANES), LANES)
            x = proj_v[:, cut].astype(F32)
            rim = rim_v[:, cut].astype(F32)[8:16] * keep
            w = short_v[:, cut]
            value = w[0:1] * x + w[1:2] * delayed(x, rim, 1) + w[2:3] * delayed(x, rim, 2)
            mix_v[part, :, cols] = value
            mixed.append(value)
        product = (mixed[1] * mixed[2]).astype(BF16)
        grad = (cot_v[:, cols].astype(F32) * mixed[0]).astype(BF16)
        both = dot(perm_v[...], jnp.concatenate([product, grad], axis=1))
        p, g = both[:, :LANES], both[:, LANES:]
        low = low_lanes(256)
        even = jnp.where(low, p, pltpu.roll(g, HALF, 1))
        odd = jnp.where(low, pltpu.roll(p, HALF, 1), g)
        send_v[2 * tile] = even.astype(BF16).reshape(16, 16, LANES)
        send_v[2 * tile + 1] = odd.astype(BF16).reshape(16, 16, LANES)
        for core in range(2):

            @pl.when(2 * tile + core != me)
            def _():
                forward_copy(2 * tile + core, me).start()

        return carry

    lax.fori_loop(1, 9, gate_tile, 0)
    own = pltpu.make_async_copy(
        send_v.at[me], recv_v.at[:, pl.ds(pl.multiple_of(me * 16, 16), 16), :], local_sem.at[0]
    )
    own.start()

    def first_stage(source, pair, carry):
        x = jnp.concatenate([source[2 * pair], source[2 * pair + 1]], axis=1)
        y = dot(first_v[...], x).astype(BF16)
        y_v[2 * pair] = y[:, :LANES]
        y_v[2 * pair + 1] = y[:, LANES:]
        return carry

    def second_stage(group):
        rows = y_v[:, pl.ds(pl.multiple_of(group * 16, 16), 16), :].reshape(256, LANES)
        return dot(second_v[group], rows)

    for load in loads[4:7]:
        load.wait()

    def filter_rows(block, carry):
        x = filt_v[:, pl.ds(pl.multiple_of(block * 256, 256), 256)].astype(BF16)
        x = jnp.concatenate([x, x], axis=0)
        x = lax.dot_general(perm_v[...], x, (((1,), (1,)), ((), ())), preferred_element_type=F32)
        x = x.astype(BF16).reshape(16, 16, LANES)
        fx_v[:, pl.ds(pl.multiple_of(block * 16, 16), 16), :] = x
        return carry

    def filter_group(group, carry):
        spec = second_stage(group)
        fs_v[group, :LANES] = spec[:LANES]
        fs_v[group, LANES:] = jnp.where(low_lanes(LANES), spec[LANES:], -spec[LANES:])
        return carry

    lax.fori_loop(0, 16, filter_rows, 0)
    lax.fori_loop(0, 8, functools.partial(first_stage, fx_v), 0)
    lax.fori_loop(0, GROUPS, filter_group, 0, unroll=UNROLL)
    for load in loads[7:]:
        load.wait()

    own.wait()

    whole_forward = pltpu.make_async_remote_copy(
        src_ref=send_v.at[pl.ds(0, 15)], dst_ref=recv_v.at[:, pl.ds(0, 240), :],
        send_sem=a_ss.at[0], recv_sem=a_rs.at[0], device_id={"ctx": nxt}, device_id_type=MESH,
    )
    whole_forward.wait_recv()

    lax.fori_loop(0, 8, functools.partial(first_stage, recv_v), 0)

    def middle_group(group, carry):
        spec = second_stage(group)
        spec_v[group] = spec.astype(BF16)
        sr, si = spec[:LANES], spec[LANES:]
        fr, fi = fs_v[group, :LANES], fs_v[group, LANES:]
        freq = jnp.concatenate([sr * fr - si * fi, sr * fi + si * fr], axis=0).astype(BF16)
        back = dot(secondt_v[group], freq).astype(BF16).reshape(16, 16, LANES)
        z_v[:, pl.ds(pl.multiple_of(group * 16, 16), 16), :] = back
        return carry

    lax.fori_loop(0, GROUPS, middle_group, 0, unroll=UNROLL)

    def last_stage(pair, carry):
        both = jnp.concatenate([z_v[2 * pair], z_v[2 * pair + 1]], axis=1)
        both = dot(firstt_v[...], both).astype(BF16)
        ysend_v[2 * pair] = both[:, :LANES]
        ysend_v[2 * pair + 1] = both[:, LANES:]
        return carry

    def back_copy(to, source, half):
        return pltpu.make_async_remote_copy(
            src_ref=ysend_v.at[pl.ds(half * 8, 8), pl.ds(pl.multiple_of(to * 16, 16), 16), :],
            dst_ref=brecv_v.at[source, pl.ds(half * 8, 8)],
            send_sem=b_ss.at[0], recv_sem=b_rs.at[source], device_id={"ctx": to}, device_id_type=MESH,
        )

    def whole_back(source):
        return pltpu.make_async_remote_copy(
            src_ref=ysend_v.at[:, pl.ds(0, 240), :], dst_ref=brecv_v.at[source],
            send_sem=b_ss.at[0], recv_sem=b_rs.at[source], device_id={"ctx": nxt}, device_id_type=MESH,
        )

    for half in range(2):
        lax.fori_loop(4 * half, 4 * half + 4, last_stage, 0)

        def send_back(step, carry, half=half):
            back_copy(lax.rem(me + step, 16), me, half).start()
            return carry

        lax.fori_loop(1, 16, send_back, 0)

    own_back = pltpu.make_async_copy(
        ysend_v.at[:, pl.ds(pl.multiple_of(me * 16, 16), 16), :], brecv_v.at[me], local_sem.at[1]
    )
    own_back.start()
    def cross_group(group, carry):
        spec = spec_v[group].astype(F32)
        sr, si = spec[:LANES], spec[LANES:]
        rr, ri = pltpu.roll(sr, HALF, 1), pltpu.roll(si, HALF, 1)
        cross = ri * sr - rr * si
        cross = jnp.where(low_lanes(LANES), cross, -cross)
        freq = jnp.concatenate([sr * rr + si * ri, cross], axis=0).astype(BF16)
        back = dot(secondt_v[group], freq).astype(BF16).reshape(16, 16, LANES)
        y_v[:, pl.ds(pl.multiple_of(group * 16, 16), 16), :] = back
        return carry

    def cross_last(pair, carry):
        both = jnp.concatenate([y_v[2 * pair], y_v[2 * pair + 1]], axis=1)
        both = dot(firstt_v[...], both)
        grad = jnp.where(low_lanes(256), both[:, :LANES], both[:, LANES:]) * scale
        fsend_v[pair] = grad.astype(BF16)
        return carry

    lax.fori_loop(0, GROUPS, cross_group, 0, unroll=UNROLL)
    lax.fori_loop(0, 8, cross_last, 0)
    row_y, low_x = dpi // 2, lax.rem(dpi, 2)

    def filter_copy(to, source):
        return pltpu.make_async_remote_copy(
            src_ref=fsend_v.at[:, pl.ds(pl.multiple_of(to * 64, 64), 64), :], dst_ref=frecv_v.at[source],
            send_sem=f_ss.at[0], recv_sem=f_rs.at[0], device_id={"dp": 2 * to + low_x}, device_id_type=MESH,
        )

    for step in range(1, 4):
        filter_copy(lax.rem(row_y + step, 4), row_y).start()
    own_filter = pltpu.make_async_copy(
        fsend_v.at[:, pl.ds(pl.multiple_of(row_y * 64, 64), 64), :], frecv_v.at[row_y], local_sem.at[2]
    )
    own_filter.start()
    own_back.wait()
    own_filter.wait()
    whole_filter = pltpu.make_async_remote_copy(
        src_ref=fsend_v.at[:, pl.ds(0, 192), :], dst_ref=frecv_v.at[pl.ds(0, 3)],
        send_sem=f_ss.at[0], recv_sem=f_rs.at[0], device_id={"dp": dpi}, device_id_type=MESH,
    )
    half_filter = pltpu.make_async_remote_copy(
        src_ref=hsend_v, dst_ref=hrecv_v, send_sem=h_ss.at[0], recv_sem=h_rs.at[0],
        device_id={"dp": dpi + 1 - 2 * low_x}, device_id_type=MESH,
    )

    def filter_sum(pair, start):
        rows = pl.ds(pl.multiple_of(start, 32), 32)
        value = frecv_v[0, pair, rows, :].astype(F32)
        for at in range(1, 4):
            value = value + frecv_v[at, pair, rows, :].astype(F32)
        return value

    def filter_half(pair, carry):
        hsend_v[pair] = filter_sum(pair, 32 - 32 * low_x).astype(BF16)
        return carry

    def rim_back_copy(tile, to):
        return pltpu.make_async_remote_copy(
            src_ref=rsend_v.at[tile], dst_ref=rrecv_v.at[tile], send_sem=r_ss.at[0], recv_sem=r_rs.at[0],
            device_id={"ctx": to}, device_id_type=MESH,
        )

    def sum_copy(to, source):
        return pltpu.make_async_remote_copy(
            src_ref=asend_v.at[to], dst_ref=arecv_v.at[source], send_sem=s_ss.at[0], recv_sem=s_rs.at[0],
            device_id={"ctx": to}, device_id_type=MESH,
        )

    def down(x):
        return jnp.sum(x, axis=0, keepdims=True)

    def grad_tile(step, carry):
        tile = lax.rem(chip + 8 - step, 8)
        cols = pl.ds(pl.multiple_of(tile * LANES, LANES), LANES)
        for core in range(2):

            @pl.when(2 * tile + core != me)
            def _():
                whole_back(2 * tile + core).wait_recv()

        pair = jnp.concatenate(
            [brecv_v[2 * tile].reshape(256, LANES), brecv_v[2 * tile + 1].reshape(256, LANES)], axis=1
        )
        pair = dot(unperm_v[...], pair)
        even, odd = pair[:, :LANES], pair[:, LANES:]
        low = low_lanes(256)
        long_part = jnp.where(low, even, pltpu.roll(odd, HALF, 1))
        back_part = jnp.where(low, pltpu.roll(even, HALF, 1), odd)
        queries, keys, values = (mix_v[part, :, cols] for part in range(3))
        cot = cot_v[:, cols].astype(F32)
        gain = skip_v[:, cols]
        product = (keys * values).astype(BF16).astype(F32)
        grad = (cot * queries).astype(BF16).astype(F32)
        gated = long_part + gain * product
        out_v[:, cols] = (queries * gated).astype(BF16)
        product_grad = back_part + gain * grad
        for part, mixed_grad in enumerate((cot * gated, product_grad * values, product_grad * keys)):
            cut = pl.ds(pl.multiple_of(tile * LANES + part * 1024, LANES), LANES)
            rounded = mixed_grad.astype(BF16)
            rsend_v[tile, 16 * part : 16 * part + 16] = rounded[:16]
            mg = rounded.astype(F32)
            one, two = advanced(mg, 1), advanced(mg, 2)
            w = short_v[:, cut]
            value = w[0:1] * mg + w[1:2] * one + w[2:3] * two
            pg_v[:, cut] = value.astype(BF16)
            tail_v[tile, 16 * part : 16 * part + 16] = value[240:]
            x = proj_v[:, cut].astype(F32)
            rim = rim_v[:, cut].astype(F32)[8:16] * keep
            head = mg[:8]
            sums = [
                down(mg * x),
                down(one * x) + head[0:1] * rim[7:8],
                down(two * x) + head[0:1] * rim[6:7] + head[1:2] * rim[7:8],
            ]
            for tap in range(3):
                at = 3 * part + tap
                asend_v[2 * tile + at // 8, at % 8 : at % 8 + 1] = sums[tap]
        asend_v[2 * tile + 1, 1:2] = down(grad * product)
        rim_back_copy(tile, prv).start()
        for core in range(2):

            @pl.when(2 * tile + core != me)
            def _():
                sum_copy(2 * tile + core, me).start()

        return carry

    lax.fori_loop(1, 9, grad_tile, 0)
    arecv_v[me] = asend_v[me]
    whole_filter.wait_recv()
    lax.fori_loop(0, 8, filter_half, 0)
    half_filter.start()
    whole_sums = pltpu.make_async_remote_copy(
        src_ref=asend_v.at[pl.ds(0, 15)], dst_ref=arecv_v.at[pl.ds(0, 15)],
        send_sem=s_ss.at[0], recv_sem=s_rs.at[0], device_id={"ctx": nxt}, device_id_type=MESH,
    )
    whole_sums.wait_recv()
    total = arecv_v[0]
    for at in range(1, 16):
        total = total + arecv_v[at]
    dsend_v[...] = jnp.broadcast_to(total[None], dsend_v.shape)
    drecv_v[dpi] = total

    def part_copy(to, source):
        return pltpu.make_async_remote_copy(
            src_ref=dsend_v.at[0], dst_ref=drecv_v.at[source], send_sem=d_ss.at[0], recv_sem=d_rs.at[0],
            device_id={"dp": to}, device_id_type=MESH,
        )

    def all_copy(to, source):
        return pltpu.make_async_remote_copy(
            src_ref=gsend_v.at[0], dst_ref=grecv_v.at[source], send_sem=g_ss.at[0], recv_sem=g_rs.at[0],
            device_id={"ctx": to}, device_id_type=MESH,
        )

    for step in range(1, 8):
        part_copy(lax.rem(dpi + step, 8), dpi).start()

    keep_back = jnp.where(me == 15, 0.0, 1.0).astype(F32)
    whole_rims = pltpu.make_async_remote_copy(
        src_ref=rsend_v, dst_ref=rrecv_v, send_sem=r_ss.at[0], recv_sem=r_rs.at[0],
        device_id={"ctx": prv}, device_id_type=MESH,
    )
    whole_rims.wait_recv()

    def fix_tile(tile, carry):
        row = lax.broadcasted_iota(jnp.int32, (16, LANES), 0)
        for part in range(3):
            cut = pl.ds(pl.multiple_of(tile * LANES + part * 1024, LANES), LANES)
            rim = rrecv_v[tile, 16 * part : 16 * part + 16].astype(F32) * keep_back
            w = short_v[:, cut]
            value = tail_v[tile, 16 * part : 16 * part + 16]
            value = value + jnp.where(row == 15, w[1:2] * rim[0:1] + w[2:3] * rim[1:2], 0.0)
            value = value + jnp.where(row == 14, w[2:3] * rim[0:1], 0.0)
            pg_v[pl.ds(240, 16), cut] = value.astype(BF16)
        return carry

    lax.fori_loop(0, 8, fix_tile, 0)

    whole_parts = pltpu.make_async_remote_copy(
        src_ref=dsend_v.at[pl.ds(0, 7)], dst_ref=drecv_v.at[pl.ds(0, 7)],
        send_sem=d_ss.at[0], recv_sem=d_rs.at[0], device_id={"ctx": nxt}, device_id_type=MESH,
    )
    whole_parts.wait_recv()
    total = drecv_v[0]
    for at in range(1, 8):
        total = total + drecv_v[at]
    total = total * scale
    gsend_v[0] = total
    grecv_v[me] = total
    for step in range(1, 16):
        all_copy(lax.rem(me + step, 16), me).start()

    half_filter.wait_recv()
    for pair in range(8):
        value = filter_sum(pair, 32 * low_x) + hrecv_v[pair].astype(F32)
        wide_v[pl.ds(2 * pair, 32, 16), :] = value
        wide_v[pl.ds(2 * pair + 1, 32, 16), :] = pltpu.roll(value, HALF, 1)
    fg_v[...] = jnp.transpose(wide_v[...])[:HALF]

    whole_forward.wait_send()
    whole_back(me).wait_send()
    whole_filter.wait_send()
    half_filter.wait_send()
    whole_rims.wait_send()
    whole_sums.wait_send()
    whole_parts.wait_send()
    whole_all = pltpu.make_async_remote_copy(
        src_ref=gsend_v.at[pl.ds(0, 15)], dst_ref=grecv_v.at[pl.ds(0, 15)],
        send_sem=g_ss.at[0], recv_sem=g_rs.at[0], device_id={"ctx": nxt}, device_id_type=MESH,
    )
    whole_all.wait_recv()
    for tile in range(8):
        for at in range(9):
            part, tap = at // 3, at % 3
            left = part * 1024 + tile * LANES
            sg_v[tap : tap + 1, left : left + LANES] = grecv_v[2 * tile + at // 8, at % 8 : at % 8 + 1]
        skg_v[:, tile * LANES : tile * LANES + LANES] = grecv_v[2 * tile + 1, 1:2]
    whole_all.wait_send()


def shards(proj, short_w, filt, skip_gain, cotangent):
    width = skip_gain.shape[0]
    scale = 1.0 / math.sqrt(proj.shape[0] * lax.axis_size("dp") * lax.axis_size("ctx"))
    whole = pl.BlockSpec(memory_space=pl.ANY)
    inside = pl.BlockSpec(memory_space=pltpu.VMEM)
    dma = pltpu.SemaphoreType.DMA
    outs = pl.pallas_call(
        functools.partial(kernel, scale),
        out_shape=[
            pltpu.VMEM((256, 1024), BF16),
            pltpu.VMEM((256, 3072), BF16),
            pltpu.VMEM((3, 3072), F32),
            pltpu.VMEM((1, 1024), F32),
            pltpu.VMEM((HALF, 512), F32),
        ],
        in_specs=[whole] * 11,
        out_specs=[inside] * 5,
        scratch_shapes=[
            pltpu.VMEM((256, 3072), BF16),
            pltpu.VMEM((256, 1024), BF16),
            pltpu.VMEM((HALF, 4096), F32),
            pltpu.VMEM((3, 3072), F32),
            pltpu.VMEM((1, 1024), F32),
            pltpu.VMEM((256, 256), BF16),
            pltpu.VMEM((256, 256), BF16),
            pltpu.VMEM((2 * HI, HI), BF16),
            pltpu.VMEM((GROUPS, 256, 256), BF16),
            pltpu.VMEM((HI, 2 * HI), BF16),
            pltpu.VMEM((GROUPS, 256, 256), BF16),
            pltpu.VMEM((16, 3072), BF16),
            pltpu.VMEM((3, 256, 1024), F32),
            pltpu.VMEM((16, 16, 16, LANES), BF16),
            pltpu.VMEM((LO, HI, LANES), BF16),
            pltpu.VMEM((LO, HI, LANES), BF16),
            pltpu.VMEM((LO, 2 * HI, LANES), BF16),
            pltpu.VMEM((GROUPS, 256, LANES), F32),
            pltpu.VMEM((GROUPS, 256, LANES), BF16),
            pltpu.VMEM((LO, 2 * HI, LANES), BF16),
            pltpu.VMEM((LO, HI, LANES), BF16),
            pltpu.VMEM((16, LO, 16, LANES), BF16),
            pltpu.VMEM((8, HI, LANES), BF16),
            pltpu.VMEM((4, 8, 64, LANES), BF16),
            pltpu.VMEM((8, 32, LANES), BF16),
            pltpu.VMEM((8, 32, LANES), BF16),
            pltpu.VMEM((8, 48, LANES), F32),
            pltpu.VMEM((8, 48, LANES), BF16),
            pltpu.VMEM((8, 48, LANES), BF16),
            pltpu.VMEM((16, 8, LANES), F32),
            pltpu.VMEM((16, 8, LANES), F32),
            pltpu.VMEM((8, 8, LANES), F32),
            pltpu.VMEM((8, 8, LANES), F32),
            pltpu.VMEM((16, 8, LANES), F32),
            pltpu.VMEM((16, 8, LANES), F32),
            pltpu.VMEM((512, LANES), F32),
            dma((11,)),
            dma((1,)), dma((1,)), dma((1,)), dma((1,)), dma((1,)), dma((16,)), dma((1,)), dma((1,)),
            dma((1,)), dma((1,)), dma((1,)), dma((1,)), dma((1,)), dma((1,)), dma((1,)), dma((1,)),
            dma((1,)), dma((1,)), dma((3,)),
        ],
        compiler_params=pltpu.CompilerParams(
            collective_id=0, has_side_effects=True, vmem_limit_bytes=56 * 1024 * 1024
        ),
    )(proj, cotangent, filt.T, short_w, skip_gain.reshape(1, width), *tables())
    outputs, proj_grad, short_grad, skip_grad, filt_grad = outs
    return (outputs, proj_grad, short_grad, skip_grad.reshape(width), filt_grad.T)


def solution(mesh):
    placed = (P(("dp", "ctx"), None), P(), P(None, "ctx"), P(), P(("dp", "ctx"), None))
    return jax.shard_map(
        shards,
        mesh=mesh,
        in_specs=placed,
        out_specs=(P(("dp", "ctx"), None), P(("dp", "ctx"), None), P(), P(), P("dp", "ctx")),
        check_vma=False,
    )
```

```python
import functools
import math

import jax
import jax.numpy as jnp
import ml_dtypes
import numpy as np
from jax import lax
from jax.experimental import pallas as pl
from jax.experimental.pallas import tpu as pltpu
from jax.sharding import PartitionSpec as P

HI = 256
LO = 16
GROUP = 8
GROUPS = HI // GROUP
UNROLL = 4
U1 = 8
U2 = 4
U3 = 16
LANES = 128
HALF = 64
MESH = pl.DeviceIdType.MESH
F32 = jnp.float32
BF16 = jnp.bfloat16


def tables():
    total = HI * LO
    start = np.arange(HI)
    angle = 2.0 * math.pi / HI * ((start[:, None] + 0.25) * np.arange(HI)[None, :] % HI)
    first = np.stack([np.cos(angle), -np.sin(angle)])
    first = first.reshape(2, GROUPS, GROUP, HI).transpose(1, 0, 2, 3).reshape(2 * HI, HI)
    freq = HI * np.arange(LO)[None, None, :] + start.reshape(GROUPS, GROUP)[:, :, None] + 0.25
    angle = 2.0 * math.pi / total * (freq[..., None] * np.arange(LO) % total)
    second = np.zeros((GROUPS, 2, LO, GROUP, LO, 2, GROUP))
    for at in range(GROUP):
        second[:, 0, :, at, :, 0, at] = np.cos(angle[:, at])
        second[:, 0, :, at, :, 1, at] = np.sin(angle[:, at])
        second[:, 1, :, at, :, 0, at] = -np.sin(angle[:, at])
        second[:, 1, :, at, :, 1, at] = np.cos(angle[:, at])
    second = second.reshape(GROUPS, 2 * LO * GROUP, 2 * LO * GROUP)
    rows = np.arange(256)
    perm = np.zeros((256, 256))
    perm[rows, rows % 16 * LO + rows // 16] = 1.0
    return [
        table.astype(ml_dtypes.bfloat16)
        for table in (perm, perm.T, first, second, first.T / total, second.transpose(0, 2, 1))
    ]


def dot(left, right):
    return jnp.dot(left, right, preferred_element_type=F32)


def low_lanes(rows):
    return lax.broadcasted_iota(jnp.int32, (rows, LANES), 1) < HALF


def delayed(x, rim, steps):
    turned = pltpu.roll(x, steps, 0)
    before = pltpu.roll(rim, steps, 0)
    row = lax.broadcasted_iota(jnp.int32, (8, LANES), 0)
    return jnp.concatenate([jnp.where(row < steps, before, turned[:8]), turned[8:]], axis=0)


def advanced(x, rim, steps):
    rows = x.shape[0]
    turned = pltpu.roll(x, rows - steps, 0)
    after = pltpu.roll(rim, 8 - steps, 0)
    row = lax.broadcasted_iota(jnp.int32, (8, LANES), 0)
    return jnp.concatenate(
        [turned[: rows - 8], jnp.where(row < 8 - steps, turned[rows - 8 :], after)], axis=0
    )


def kernel(
    scale,
    proj_h, cot_h, filt_h, short_h, skip_h, perm_h, unperm_h, first_h, second_h, firstt_h, secondt_h,
    out_v, pg_v, grecv_v, fg_v,
    proj_v, cot_v, filt_v, short_v, skip_v, perm_v, unperm_v, first_v, second_v, firstt_v, secondt_v,
    rim_v, mix_v, send_v, recv_v, fx_v, y_v, fs_v, spec_v, z_v, ysend_v, brecv_v, fsend_v, frecv_v, hsend_v, hrecv_v,
    xs_v, ready_v, mg_v, rsend_v, rrecv_v, asend_v, arecv_v, dsend_v, drecv_v, gsend_v, wide_v,
    load_sem, rim_ss, rim_rs, a_ss, a_rs, b_ss, b_rs, f_ss, f_rs, h_ss, h_rs, r_ss, r_rs, s_ss, s_rs, d_ss, d_rs,
    g_ss, g_rs, local_sem,
):
    me = lax.axis_index("ctx")
    dpi = lax.axis_index("dp")
    chip = me // 2
    nxt = lax.rem(me + 1, 16)
    prv = lax.rem(me + 15, 16)

    barrier = pltpu.get_barrier_semaphore()
    for step in range(1, 16):
        pl.semaphore_signal(
            barrier, inc=1, device_id={"ctx": lax.rem(me + step, 16)}, device_id_type=MESH
        )
    for step in range(1, 8):
        pl.semaphore_signal(
            barrier, inc=1, device_id={"dp": lax.rem(dpi + step, 8)}, device_id_type=MESH
        )

    loads = [
        pltpu.make_async_copy(src, dst, load_sem.at[at])
        for at, (src, dst) in enumerate(
            [
                (proj_h, proj_v), (cot_h, cot_v), (short_h, short_v), (perm_h, perm_v), (filt_h, filt_v),
                (first_h, first_v), (second_h, second_v), (secondt_h, secondt_v), (firstt_h, firstt_v),
                (unperm_h, unperm_v), (skip_h, skip_v),
            ]
        )
    ]
    for load in loads[:4]:
        load.start()
    asend_v[...] = jnp.zeros_like(asend_v)
    pl.semaphore_wait(barrier, 22)

    def rim_copy(to):
        return pltpu.make_async_remote_copy(
            src_ref=proj_h.at[pl.ds(240, 16), :], dst_ref=rim_v, send_sem=rim_ss.at[0], recv_sem=rim_rs.at[0],
            device_id={"ctx": to}, device_id_type=MESH,
        )

    rim_copy(nxt).start()
    for load in loads[:4]:
        load.wait()
    for load in loads[4:]:
        load.start()
    keep = jnp.where(me == 0, 0.0, 1.0).astype(F32)

    def forward_copy(to, source, start, count):
        return pltpu.make_async_remote_copy(
            src_ref=send_v.at[to, pl.ds(start, count)],
            dst_ref=recv_v.at[pl.ds(start, count), pl.ds(pl.multiple_of(source * 16, 16), 16), :],
            send_sem=a_ss.at[0], recv_sem=a_rs.at[0], device_id={"ctx": to}, device_id_type=MESH,
        )

    def gate_tile(step, carry):
        tile = lax.rem(chip + step, 8)
        cols = pl.ds(pl.multiple_of(tile * LANES, LANES), LANES)
        mixed = []
        for part in range(3):
            cut = pl.ds(pl.multiple_of(tile * LANES + part * 1024, LANES), LANES)
            x = proj_v[:, cut].astype(F32)
            w = short_v[:, cut]
            value = w[0:1] * x + w[1:2] * pltpu.roll(x, 1, 0) + w[2:3] * pltpu.roll(x, 2, 0)
            mix_v[part, :, cols] = value
            mixed.append(value)
        product = (mixed[1] * mixed[2]).astype(BF16)
        grad = (cot_v[:, cols].astype(F32) * mixed[0]).astype(BF16)
        both = dot(perm_v[...], jnp.concatenate([product, grad], axis=1))
        p, g = both[:, :LANES], both[:, LANES:]
        low = low_lanes(256)
        even = jnp.where(low, p, pltpu.roll(g, HALF, 1))
        odd = jnp.where(low, pltpu.roll(p, HALF, 1), g)
        send_v[2 * tile] = even.astype(BF16).reshape(16, 16, LANES)
        send_v[2 * tile + 1] = odd.astype(BF16).reshape(16, 16, LANES)
        for core in range(2):

            @pl.when(2 * tile + core != me)
            def _():
                forward_copy(2 * tile + core, me, 2, 14).start()

        return carry

    def gate_head(step, carry):
        tile = lax.rem(chip + step, 8)
        cols = pl.ds(pl.multiple_of(tile * LANES, LANES), LANES)
        mixed = []
        for part in range(3):
            cut = pl.ds(pl.multiple_of(tile * LANES + part * 1024, LANES), LANES)
            x = proj_v[pl.ds(0, 16), cut].astype(F32)
            rim = rim_v[:, cut].astype(F32)[8:16] * keep
            w = short_v[:, cut]
            value = (w[0:1] * x + w[1:2] * delayed(x, rim, 1) + w[2:3] * delayed(x, rim, 2))[:8]
            mix_v[part, pl.ds(0, 8), cols] = value
            mixed.append(value)
        p = (mixed[1] * mixed[2]).astype(BF16).astype(F32)
        g = (cot_v[pl.ds(0, 16), cols].astype(F32)[:8] * mixed[0]).astype(BF16).astype(F32)
        low = low_lanes(8)
        row = lax.broadcasted_iota(jnp.int32, (16, LANES), 0)
        for core, head in enumerate(
            (jnp.where(low, p, pltpu.roll(g, HALF, 1)), jnp.where(low, pltpu.roll(p, HALF, 1), g))
        ):
            for at in range(2):
                block = send_v[2 * tile + core, at].astype(F32)
                block = jnp.where(row == 0, head[at : at + 1], block)
                send_v[2 * tile + core, at] = block.astype(BF16)

            @pl.when(2 * tile + core != me)
            def _():
                forward_copy(2 * tile + core, me, 0, 2).start()

        return carry

    lax.fori_loop(1, 9, gate_tile, 0)
    rim_copy(nxt).wait()
    lax.fori_loop(1, 9, gate_head, 0)
    own = pltpu.make_async_copy(
        send_v.at[me], recv_v.at[:, pl.ds(pl.multiple_of(me * 16, 16), 16), :], local_sem.at[0]
    )
    own.start()

    def first_stage(source, pair, carry):
        x = jnp.concatenate([source[2 * pair], source[2 * pair + 1]], axis=1)
        y = dot(first_v[...], x).astype(BF16)
        y_v[2 * pair] = y[:, :LANES]
        y_v[2 * pair + 1] = y[:, LANES:]
        return carry

    def second_stage(group):
        rows = y_v[:, pl.ds(pl.multiple_of(group * 16, 16), 16), :].reshape(256, LANES)
        return dot(second_v[group], rows)

    for load in loads[4:7]:
        load.wait()

    def filter_rows(block, carry):
        x = filt_v[:, pl.ds(pl.multiple_of(block * 256, 256), 256)].astype(BF16)
        x = jnp.concatenate([x, x], axis=0)
        x = lax.dot_general(perm_v[...], x, (((1,), (1,)), ((), ())), preferred_element_type=F32)
        x = x.astype(BF16).reshape(16, 16, LANES)
        fx_v[:, pl.ds(pl.multiple_of(block * 16, 16), 16), :] = x
        return carry

    def filter_group(group, carry):
        spec = second_stage(group)
        fs_v[group, :LANES] = spec[:LANES]
        fs_v[group, LANES:] = jnp.where(low_lanes(LANES), spec[LANES:], -spec[LANES:])
        return carry

    lax.fori_loop(0, 16, filter_rows, 0)
    lax.fori_loop(0, 8, functools.partial(first_stage, fx_v), 0)
    lax.fori_loop(0, GROUPS, filter_group, 0, unroll=UNROLL)
    for load in loads[7:]:
        load.wait()

    own.wait()

    whole_forward = pltpu.make_async_remote_copy(
        src_ref=send_v.at[pl.ds(0, 15)], dst_ref=recv_v.at[:, pl.ds(0, 240), :],
        send_sem=a_ss.at[0], recv_sem=a_rs.at[0], device_id={"ctx": nxt}, device_id_type=MESH,
    )
    whole_forward.wait_recv()

    lax.fori_loop(0, 8, functools.partial(first_stage, recv_v), 0, unroll=U1)

    def middle_group(group, carry):
        spec = second_stage(group)
        spec_v[group] = spec
        sr, si = spec[:LANES], spec[LANES:]
        fr, fi = fs_v[group, :LANES], fs_v[group, LANES:]
        freq = jnp.concatenate([sr * fr - si * fi, sr * fi + si * fr], axis=0).astype(BF16)
        back = dot(secondt_v[group], freq).astype(BF16).reshape(16, 16, LANES)
        z_v[:, pl.ds(pl.multiple_of(group * 16, 16), 16), :] = back
        return carry

    lax.fori_loop(0, GROUPS, middle_group, 0, unroll=U3)

    def last_stage(pair, carry):
        both = jnp.concatenate([z_v[2 * pair], z_v[2 * pair + 1]], axis=1)
        both = dot(firstt_v[...], both).astype(BF16)
        ysend_v[2 * pair] = both[:, :LANES]
        ysend_v[2 * pair + 1] = both[:, LANES:]
        return carry

    def back_copy(to, source, half):
        return pltpu.make_async_remote_copy(
            src_ref=ysend_v.at[pl.ds(half * 8, 8), pl.ds(pl.multiple_of(to * 16, 16), 16), :],
            dst_ref=brecv_v.at[source, pl.ds(half * 8, 8)],
            send_sem=b_ss.at[0], recv_sem=b_rs.at[source], device_id={"ctx": to}, device_id_type=MESH,
        )

    def whole_back(source):
        return pltpu.make_async_remote_copy(
            src_ref=ysend_v.at[:, pl.ds(0, 240), :], dst_ref=brecv_v.at[source],
            send_sem=b_ss.at[0], recv_sem=b_rs.at[source], device_id={"ctx": nxt}, device_id_type=MESH,
        )

    for half in range(2):
        lax.fori_loop(4 * half, 4 * half + 4, last_stage, 0, unroll=U2)

        def send_back(step, carry, half=half):
            back_copy(lax.rem(me + step, 16), me, half).start()
            return carry

        lax.fori_loop(1, 16, send_back, 0)

    own_back = pltpu.make_async_copy(
        ysend_v.at[:, pl.ds(pl.multiple_of(me * 16, 16), 16), :], brecv_v.at[me], local_sem.at[1]
    )
    own_back.start()
    def cross_group(group, carry):
        spec = spec_v[group]
        sr, si = spec[:LANES], spec[LANES:]
        rr, ri = pltpu.roll(sr, HALF, 1), pltpu.roll(si, HALF, 1)
        cross = ri * sr - rr * si
        cross = jnp.where(low_lanes(LANES), cross, -cross)
        freq = jnp.concatenate([sr * rr + si * ri, cross], axis=0).astype(BF16)
        back = dot(secondt_v[group], freq).astype(BF16).reshape(16, 16, LANES)
        y_v[:, pl.ds(pl.multiple_of(group * 16, 16), 16), :] = back
        return carry

    def cross_last(pair, carry):
        both = jnp.concatenate([y_v[2 * pair], y_v[2 * pair + 1]], axis=1)
        both = dot(firstt_v[...], both)
        grad = jnp.where(low_lanes(256), both[:, :LANES], both[:, LANES:]) * scale
        fsend_v[pair] = grad.astype(BF16)
        return carry

    lax.fori_loop(0, GROUPS, cross_group, 0, unroll=UNROLL)
    lax.fori_loop(0, 8, cross_last, 0)
    row_y, low_x = dpi // 2, lax.rem(dpi, 2)

    def filter_copy(to, source):
        return pltpu.make_async_remote_copy(
            src_ref=fsend_v.at[:, pl.ds(pl.multiple_of(to * 64, 64), 64), :], dst_ref=frecv_v.at[source],
            send_sem=f_ss.at[0], recv_sem=f_rs.at[0], device_id={"dp": 2 * to + low_x}, device_id_type=MESH,
        )

    for step in range(1, 4):
        filter_copy(lax.rem(row_y + step, 4), row_y).start()
    own_filter = pltpu.make_async_copy(
        fsend_v.at[:, pl.ds(pl.multiple_of(row_y * 64, 64), 64), :], frecv_v.at[row_y], local_sem.at[2]
    )
    own_filter.start()
    own_back.wait()
    own_filter.wait()
    whole_filter = pltpu.make_async_remote_copy(
        src_ref=fsend_v.at[:, pl.ds(0, 192), :], dst_ref=frecv_v.at[pl.ds(0, 3)],
        send_sem=f_ss.at[0], recv_sem=f_rs.at[0], device_id={"dp": dpi}, device_id_type=MESH,
    )
    half_filter = pltpu.make_async_remote_copy(
        src_ref=hsend_v, dst_ref=hrecv_v, send_sem=h_ss.at[0], recv_sem=h_rs.at[0],
        device_id={"dp": dpi + 1 - 2 * low_x}, device_id_type=MESH,
    )

    def filter_sum(pair, start):
        rows = pl.ds(pl.multiple_of(start, 32), 32)
        value = frecv_v[0, pair, rows, :].astype(F32)
        for at in range(1, 4):
            value = value + frecv_v[at, pair, rows, :].astype(F32)
        return value

    def filter_half(pair, carry):
        hsend_v[pair] = filter_sum(pair, 32 - 32 * low_x).astype(BF16)
        return carry

    def rim_back_copy(tile, to):
        return pltpu.make_async_remote_copy(
            src_ref=rsend_v.at[tile], dst_ref=rrecv_v.at[tile], send_sem=r_ss.at[0], recv_sem=r_rs.at[0],
            device_id={"ctx": to}, device_id_type=MESH,
        )

    def sum_copy(to, source):
        return pltpu.make_async_remote_copy(
            src_ref=asend_v.at[to], dst_ref=arecv_v.at[source], send_sem=s_ss.at[0], recv_sem=s_rs.at[0],
            device_id={"ctx": to}, device_id_type=MESH,
        )

    def down(x):
        return jnp.sum(x, axis=0, keepdims=True)

    def ready_tile(tile, carry):
        cols = pl.ds(pl.multiple_of(tile * LANES, LANES), LANES)
        queries, keys, values = (mix_v[part, :, cols] for part in range(3))
        cot = cot_v[:, cols].astype(F32)
        gain = skip_v[:, cols]
        product = (keys * values).astype(BF16).astype(F32)
        grad = (cot * queries).astype(BF16).astype(F32)
        ready_v[0, :, cols] = gain * product
        ready_v[1, :, cols] = gain * grad
        ready_v[2, :, cols] = cot
        asend_v[2 * tile + 1, 1:2] = down(grad * product)
        for part in range(3):
            cut = pl.ds(pl.multiple_of(tile * LANES + part * 1024, LANES), LANES)
            x = proj_v[:, cut].astype(F32)
            rim = rim_v[:, cut].astype(F32)[8:16] * keep
            xs_v[0, :, cut] = delayed(x, rim, 1)
            xs_v[1, :, cut] = delayed(x, rim, 2)
        return carry

    lax.fori_loop(0, 8, ready_tile, 0)
    whole_filter.wait_recv()
    lax.fori_loop(0, 8, filter_half, 0)
    half_filter.start()

    def grad_tile(step, carry):
        tile = lax.rem(chip + 8 - step, 8)
        cols = pl.ds(pl.multiple_of(tile * LANES, LANES), LANES)
        for core in range(2):

            @pl.when(2 * tile + core != me)
            def _():
                whole_back(2 * tile + core).wait_recv()

        pair = jnp.concatenate(
            [brecv_v[2 * tile].reshape(256, LANES), brecv_v[2 * tile + 1].reshape(256, LANES)], axis=1
        )
        pair = dot(unperm_v[...], pair)
        even, odd = pair[:, :LANES], pair[:, LANES:]
        low = low_lanes(256)
        gated = jnp.where(low, even, pltpu.roll(odd, HALF, 1)) + ready_v[0, :, cols]
        product_grad = jnp.where(low, pltpu.roll(even, HALF, 1), odd) + ready_v[1, :, cols]
        queries, keys, values = (mix_v[part, :, cols] for part in range(3))
        out_v[:, cols] = (queries * gated).astype(BF16)
        for part, mixed_grad in enumerate((ready_v[2, :, cols] * gated, product_grad * values, product_grad * keys)):
            cut = pl.ds(pl.multiple_of(tile * LANES + part * 1024, LANES), LANES)
            rounded = mixed_grad.astype(BF16)
            mg_v[:, cut] = rounded
            rsend_v[tile, 16 * part : 16 * part + 16] = rounded[:16]
            mg = rounded.astype(F32)
            sums = [down(mg * x) for x in (proj_v[:, cut].astype(F32), xs_v[0, :, cut], xs_v[1, :, cut])]
            for tap in range(3):
                at = 3 * part + tap
                asend_v[2 * tile + at // 8, at % 8 : at % 8 + 1] = sums[tap]
        rim_back_copy(tile, prv).start()
        for core in range(2):

            @pl.when(2 * tile + core != me)
            def _():
                sum_copy(2 * tile + core, me).start()

        return carry

    lax.fori_loop(1, 9, grad_tile, 0)
    arecv_v[me] = asend_v[me]
    half_filter.wait_recv()
    for pair in range(8):
        value = filter_sum(pair, 32 * low_x) + hrecv_v[pair].astype(F32)
        wide_v[pl.ds(2 * pair, 32, 16), :] = value
        wide_v[pl.ds(2 * pair + 1, 32, 16), :] = pltpu.roll(value, HALF, 1)
    fg_v[...] = jnp.transpose(wide_v[...])[:HALF]
    whole_sums = pltpu.make_async_remote_copy(
        src_ref=asend_v.at[pl.ds(0, 15)], dst_ref=arecv_v.at[pl.ds(0, 15)],
        send_sem=s_ss.at[0], recv_sem=s_rs.at[0], device_id={"ctx": nxt}, device_id_type=MESH,
    )
    whole_sums.wait_recv()
    total = arecv_v[0]
    for at in range(1, 16):
        total = total + arecv_v[at]
    dsend_v[...] = jnp.broadcast_to(total[None], dsend_v.shape)
    drecv_v[dpi] = total

    def part_copy(to, source):
        return pltpu.make_async_remote_copy(
            src_ref=dsend_v.at[0], dst_ref=drecv_v.at[source], send_sem=d_ss.at[0], recv_sem=d_rs.at[0],
            device_id={"dp": to}, device_id_type=MESH,
        )

    def all_copy(to, source):
        return pltpu.make_async_remote_copy(
            src_ref=gsend_v.at[0], dst_ref=grecv_v.at[source], send_sem=g_ss.at[0], recv_sem=g_rs.at[0],
            device_id={"ctx": to}, device_id_type=MESH,
        )

    for step in range(1, 8):
        part_copy(lax.rem(dpi + step, 8), dpi).start()

    keep_back = jnp.where(me == 15, 0.0, 1.0).astype(F32)
    whole_rims = pltpu.make_async_remote_copy(
        src_ref=rsend_v, dst_ref=rrecv_v, send_sem=r_ss.at[0], recv_sem=r_rs.at[0],
        device_id={"ctx": prv}, device_id_type=MESH,
    )
    whole_rims.wait_recv()

    def last_tile(tile, carry):
        for part in range(3):
            cut = pl.ds(pl.multiple_of(tile * LANES + part * 1024, LANES), LANES)
            rim = rrecv_v[tile, 16 * part : 16 * part + 16].astype(F32)[:8] * keep_back
            mg = mg_v[:, cut].astype(F32)
            w = short_v[:, cut]
            value = w[0:1] * mg + w[1:2] * advanced(mg, rim, 1) + w[2:3] * advanced(mg, rim, 2)
            pg_v[:, cut] = value.astype(BF16)
        return carry

    lax.fori_loop(0, 4, last_tile, 0)

    whole_parts = pltpu.make_async_remote_copy(
        src_ref=dsend_v.at[pl.ds(0, 7)], dst_ref=drecv_v.at[pl.ds(0, 7)],
        send_sem=d_ss.at[0], recv_sem=d_rs.at[0], device_id={"ctx": nxt}, device_id_type=MESH,
    )
    whole_parts.wait_recv()
    total = drecv_v[0]
    for at in range(1, 8):
        total = total + drecv_v[at]
    total = total * scale
    gsend_v[0] = total
    grecv_v[me] = total
    for step in range(1, 16):
        all_copy(lax.rem(me + step, 16), me).start()

    lax.fori_loop(4, 8, last_tile, 0)
    whole_forward.wait_send()
    whole_back(me).wait_send()
    whole_filter.wait_send()
    half_filter.wait_send()
    whole_rims.wait_send()
    whole_sums.wait_send()
    whole_parts.wait_send()
    whole_all = pltpu.make_async_remote_copy(
        src_ref=gsend_v.at[pl.ds(0, 15)], dst_ref=grecv_v.at[pl.ds(0, 15)],
        send_sem=g_ss.at[0], recv_sem=g_rs.at[0], device_id={"ctx": nxt}, device_id_type=MESH,
    )
    whole_all.wait_recv()
    whole_all.wait_send()


def result_kernel(out_v, pg_v, sums_v, fg_v, out_r, pg_r, sg_r, skg_r, fg_r, sg_v, skg_v, sem):
    copies = [
        pltpu.make_async_copy(src, dst, sem.at[at])
        for at, (src, dst) in enumerate([(pg_v, pg_r), (out_v, out_r), (fg_v, fg_r), (sg_v, sg_r), (skg_v, skg_r)])
    ]
    for copy in copies[:3]:
        copy.start()
    for tile in range(8):
        for at in range(9):
            part, tap = at // 3, at % 3
            left = part * 1024 + tile * LANES
            sg_v[tap : tap + 1, left : left + LANES] = sums_v[2 * tile + at // 8, at % 8 : at % 8 + 1]
        skg_v[:, tile * LANES : tile * LANES + LANES] = sums_v[2 * tile + 1, 1:2]
    for copy in copies[3:]:
        copy.start()
    for copy in copies:
        copy.wait()


def shards(proj, short_w, filt, skip_gain, cotangent):
    width = skip_gain.shape[0]
    scale = 1.0 / math.sqrt(proj.shape[0] * lax.axis_size("dp") * lax.axis_size("ctx"))
    whole = pl.BlockSpec(memory_space=pl.ANY)
    inside = pl.BlockSpec(memory_space=pltpu.VMEM)
    dma = pltpu.SemaphoreType.DMA
    outs = pl.pallas_call(
        functools.partial(kernel, scale),
        out_shape=[
            pltpu.VMEM((256, 1024), BF16),
            pltpu.VMEM((256, 3072), BF16),
            pltpu.VMEM((16, 8, LANES), F32),
            pltpu.VMEM((HALF, 512), F32),
        ],
        in_specs=[whole] * 11,
        out_specs=[inside] * 4,
        scratch_shapes=[
            pltpu.VMEM((256, 3072), BF16),
            pltpu.VMEM((256, 1024), BF16),
            pltpu.VMEM((HALF, 4096), F32),
            pltpu.VMEM((3, 3072), F32),
            pltpu.VMEM((1, 1024), F32),
            pltpu.VMEM((256, 256), BF16),
            pltpu.VMEM((256, 256), BF16),
            pltpu.VMEM((2 * HI, HI), BF16),
            pltpu.VMEM((GROUPS, 256, 256), BF16),
            pltpu.VMEM((HI, 2 * HI), BF16),
            pltpu.VMEM((GROUPS, 256, 256), BF16),
            pltpu.VMEM((16, 3072), BF16),
            pltpu.VMEM((3, 256, 1024), F32),
            pltpu.VMEM((16, 16, 16, LANES), BF16),
            pltpu.VMEM((LO, HI, LANES), BF16),
            pltpu.VMEM((LO, HI, LANES), BF16),
            pltpu.VMEM((LO, 2 * HI, LANES), BF16),
            pltpu.VMEM((GROUPS, 256, LANES), F32),
            pltpu.VMEM((GROUPS, 256, LANES), F32),
            pltpu.VMEM((LO, 2 * HI, LANES), BF16),
            pltpu.VMEM((LO, HI, LANES), BF16),
            pltpu.VMEM((16, LO, 16, LANES), BF16),
            pltpu.VMEM((8, HI, LANES), BF16),
            pltpu.VMEM((4, 8, 64, LANES), BF16),
            pltpu.VMEM((8, 32, LANES), BF16),
            pltpu.VMEM((8, 32, LANES), BF16),
            pltpu.VMEM((2, 256, 3072), F32),
            pltpu.VMEM((3, 256, 1024), F32),
            pltpu.VMEM((256, 3072), BF16),
            pltpu.VMEM((8, 48, LANES), BF16),
            pltpu.VMEM((8, 48, LANES), BF16),
            pltpu.VMEM((16, 8, LANES), F32),
            pltpu.VMEM((16, 8, LANES), F32),
            pltpu.VMEM((8, 8, LANES), F32),
            pltpu.VMEM((8, 8, LANES), F32),
            pltpu.VMEM((16, 8, LANES), F32),
            pltpu.VMEM((512, LANES), F32),
            dma((11,)),
            dma((1,)), dma((1,)), dma((1,)), dma((1,)), dma((1,)), dma((16,)), dma((1,)), dma((1,)),
            dma((1,)), dma((1,)), dma((1,)), dma((1,)), dma((1,)), dma((1,)), dma((1,)), dma((1,)),
            dma((1,)), dma((1,)), dma((3,)),
        ],
        compiler_params=pltpu.CompilerParams(
            collective_id=0, has_side_effects=True, vmem_limit_bytes=56 * 1024 * 1024
        ),
    )(proj, cotangent, filt.T, short_w, skip_gain.reshape(1, width), *tables())
    outs = [pltpu.with_memory_space_constraint(value, pltpu.VMEM) for value in outs]
    outputs, proj_grad, short_grad, skip_grad, filt_grad = pl.pallas_call(
        result_kernel,
        out_shape=[
            jax.ShapeDtypeStruct((256, 1024), BF16),
            jax.ShapeDtypeStruct((256, 3072), BF16),
            jax.ShapeDtypeStruct((3, 3072), F32),
            jax.ShapeDtypeStruct((1, 1024), F32),
            jax.ShapeDtypeStruct((HALF, 512), F32),
        ],
        in_specs=[inside] * 4,
        out_specs=[whole] * 5,
        scratch_shapes=[pltpu.VMEM((3, 3072), F32), pltpu.VMEM((1, 1024), F32), dma((5,))],
    )(*outs)
    return (outputs, proj_grad, short_grad, skip_grad.reshape(width), filt_grad.T)


def solution(mesh):
    placed = (P(("dp", "ctx"), None), P(), P(None, "ctx"), P(), P(("dp", "ctx"), None))
    return jax.shard_map(
        shards,
        mesh=mesh,
        in_specs=placed,
        out_specs=(P(("dp", "ctx"), None), P(("dp", "ctx"), None), P(), P(), P("dp", "ctx")),
        check_vma=False,
    )
```

```python
import functools
import math

import jax
import jax.numpy as jnp
import ml_dtypes
import numpy as np
from jax import lax
from jax.experimental import pallas as pl
from jax.experimental.pallas import tpu as pltpu
from jax.sharding import PartitionSpec as P

HI = 256
LO = 16
GROUP = 8
GROUPS = HI // GROUP
UNROLL = 4
U1 = 8
U2 = 4
U3 = 16
CHUNK = 32
LANES = 128
HALF = 64
MESH = pl.DeviceIdType.MESH
F32 = jnp.float32
BF16 = jnp.bfloat16


def tables():
    total = HI * LO
    start = np.arange(HI)
    angle = 2.0 * math.pi / HI * ((start[:, None] + 0.25) * np.arange(HI)[None, :] % HI)
    first = np.stack([np.cos(angle), -np.sin(angle)])
    first = first.reshape(2, GROUPS, GROUP, HI).transpose(1, 0, 2, 3).reshape(2 * HI, HI)
    freq = HI * np.arange(LO)[None, None, :] + start.reshape(GROUPS, GROUP)[:, :, None] + 0.25
    angle = 2.0 * math.pi / total * (freq[..., None] * np.arange(LO) % total)
    second = np.zeros((GROUPS, 2, LO, GROUP, LO, 2, GROUP))
    for at in range(GROUP):
        second[:, 0, :, at, :, 0, at] = np.cos(angle[:, at])
        second[:, 0, :, at, :, 1, at] = np.sin(angle[:, at])
        second[:, 1, :, at, :, 0, at] = -np.sin(angle[:, at])
        second[:, 1, :, at, :, 1, at] = np.cos(angle[:, at])
    second = second.reshape(GROUPS, 2 * LO * GROUP, 2 * LO * GROUP)
    rows = np.arange(256)
    perm = np.zeros((256, 256))
    perm[rows, rows % 16 * LO + rows // 16] = 1.0
    return [
        table.astype(ml_dtypes.bfloat16)
        for table in (perm, perm.T, first, second, first.T / total, second.transpose(0, 2, 1))
    ]


def dot(left, right):
    return jnp.dot(left, right, preferred_element_type=F32)


def low_lanes(rows):
    return lax.broadcasted_iota(jnp.int32, (rows, LANES), 1) < HALF


def delayed(x, rim, steps):
    turned = pltpu.roll(x, steps, 0)
    before = pltpu.roll(rim, steps, 0)
    row = lax.broadcasted_iota(jnp.int32, (8, LANES), 0)
    return jnp.concatenate([jnp.where(row < steps, before, turned[:8]), turned[8:]], axis=0)


def advanced(x, rim, steps):
    rows = x.shape[0]
    turned = pltpu.roll(x, rows - steps, 0)
    after = pltpu.roll(rim, 8 - steps, 0)
    row = lax.broadcasted_iota(jnp.int32, (8, LANES), 0)
    return jnp.concatenate(
        [turned[: rows - 8], jnp.where(row < 8 - steps, turned[rows - 8 :], after)], axis=0
    )


def kernel(
    scale,
    proj_h, cot_h, filt_h, short_h, skip_h, perm_h, unperm_h, first_h, second_h, firstt_h, secondt_h,
    out_v, pg_v, grecv_v, fg_v,
    proj_v, cot_v, filt_v, short_v, skip_v, perm_v, unperm_v, first_v, second_v, firstt_v, secondt_v,
    rim_v, mix_v, send_v, recv_v, fx_v, y_v, fs_v, spec_v, z_v, ysend_v, brecv_v, fsend_v, frecv_v, hsend_v, hrecv_v,
    xs_v, ready_v, mg_v, gates_v, pair_v, rsend_v, rrecv_v, asend_v, arecv_v, dsend_v, drecv_v, gsend_v, wide_v,
    load_sem, rim_ss, rim_rs, a_ss, a_rs, b_ss, b_rs, f_ss, f_rs, h_ss, h_rs, r_ss, r_rs, s_ss, s_rs, d_ss, d_rs,
    g_ss, g_rs, local_sem,
):
    me = lax.axis_index("ctx")
    dpi = lax.axis_index("dp")
    chip = me // 2
    nxt = lax.rem(me + 1, 16)
    prv = lax.rem(me + 15, 16)

    barrier = pltpu.get_barrier_semaphore()
    for step in range(1, 16):
        pl.semaphore_signal(
            barrier, inc=1, device_id={"ctx": lax.rem(me + step, 16)}, device_id_type=MESH
        )
    side, seat = me // 8, lax.rem(me, 8)
    line = side * 8 + dpi

    def line_id(at):
        return {"dp": lax.rem(at, 8), "ctx": at // 8 * 8 + seat}

    for step in (1, 2, 3, 4, 5, 6, 7, 9, 10, 11, 12, 13, 14, 15):
        pl.semaphore_signal(
            barrier, inc=1, device_id=line_id((side if step < 8 else 1 - side) * 8 +
            lax.rem(dpi + step, 8)), device_id_type=MESH,
        )

    loads = [
        pltpu.make_async_copy(src, dst, load_sem.at[at])
        for at, (src, dst) in enumerate(
            [
                (proj_h, proj_v), (cot_h, cot_v), (short_h, short_v), (perm_h, perm_v), (filt_h, filt_v),
                (first_h, first_v), (second_h, second_v), (secondt_h, secondt_v), (firstt_h, firstt_v),
                (unperm_h, unperm_v), (skip_h, skip_v),
            ]
        )
    ]
    for load in loads[:4]:
        load.start()
    asend_v[...] = jnp.zeros_like(asend_v)
    pl.semaphore_wait(barrier, 29)

    def rim_copy(to):
        return pltpu.make_async_remote_copy(
            src_ref=proj_h.at[pl.ds(240, 16), :], dst_ref=rim_v, send_sem=rim_ss.at[0], recv_sem=rim_rs.at[0],
            device_id={"ctx": to}, device_id_type=MESH,
        )

    rim_copy(nxt).start()
    for load in loads[:4]:
        load.wait()
    for load in loads[4:]:
        load.start()
    keep = jnp.where(me == 0, 0.0, 1.0).astype(F32)

    def forward_copy(to, source, start, count):
        return pltpu.make_async_remote_copy(
            src_ref=send_v.at[to, pl.ds(start, count)],
            dst_ref=recv_v.at[pl.ds(start, count), pl.ds(pl.multiple_of(source * 16, 16), 16), :],
            send_sem=a_ss.at[0], recv_sem=a_rs.at[0], device_id={"ctx": to}, device_id_type=MESH,
        )

    def earlier(cut, top, rim=None):
        x = proj_v[pl.ds(top, CHUNK), cut].astype(F32)
        before = proj_v[pl.ds(top - 16, 16), cut].astype(F32)[8:] if top else rim
        if before is None:
            before = jnp.zeros((8, LANES), F32)
        return delayed(x, before, 1), delayed(x, before, 2), x

    def gate_tile(step, carry):
        tile = lax.rem(chip + step, 8)
        cols = pl.ds(pl.multiple_of(tile * LANES, LANES), LANES)
        for top in range(0, 256, CHUNK):
            rows = pl.ds(top, CHUNK)
            mixed = []
            for part in range(3):
                cut = pl.ds(pl.multiple_of(tile * LANES + part * 1024, LANES), LANES)
                one, two, x = earlier(cut, top)
                w = short_v[:, cut]
                value = w[0:1] * x + w[1:2] * one + w[2:3] * two
                mix_v[part, rows, cols] = value
                mixed.append(value)
            gates_v[rows, :LANES] = (mixed[1] * mixed[2]).astype(BF16)
            gates_v[rows, LANES:] = (cot_v[rows, cols].astype(F32) * mixed[0]).astype(BF16)
        both = dot(perm_v[...], gates_v[...])
        p, g = both[:, :LANES], both[:, LANES:]
        low = low_lanes(256)
        even = jnp.where(low, p, pltpu.roll(g, HALF, 1))
        odd = jnp.where(low, pltpu.roll(p, HALF, 1), g)
        send_v[2 * tile] = even.astype(BF16).reshape(16, 16, LANES)
        send_v[2 * tile + 1] = odd.astype(BF16).reshape(16, 16, LANES)
        for core in range(2):

            @pl.when(2 * tile + core != me)
            def _():
                forward_copy(2 * tile + core, me, 2, 14).start()

        return carry

    def gate_head(step, carry):
        tile = lax.rem(chip + step, 8)
        cols = pl.ds(pl.multiple_of(tile * LANES, LANES), LANES)
        mixed = []
        for part in range(3):
            cut = pl.ds(pl.multiple_of(tile * LANES + part * 1024, LANES), LANES)
            x = proj_v[pl.ds(0, 16), cut].astype(F32)
            rim = rim_v[:, cut].astype(F32)[8:16] * keep
            w = short_v[:, cut]
            value = (w[0:1] * x + w[1:2] * delayed(x, rim, 1) + w[2:3] * delayed(x, rim, 2))[:8]
            mix_v[part, pl.ds(0, 8), cols] = value
            mixed.append(value)
        p = (mixed[1] * mixed[2]).astype(BF16).astype(F32)
        g = (cot_v[pl.ds(0, 16), cols].astype(F32)[:8] * mixed[0]).astype(BF16).astype(F32)
        low = low_lanes(8)
        row = lax.broadcasted_iota(jnp.int32, (16, LANES), 0)
        for core, head in enumerate(
            (jnp.where(low, p, pltpu.roll(g, HALF, 1)), jnp.where(low, pltpu.roll(p, HALF, 1), g))
        ):
            for at in range(2):
                block = send_v[2 * tile + core, at].astype(F32)
                block = jnp.where(row == 0, head[at : at + 1], block)
                send_v[2 * tile + core, at] = block.astype(BF16)

            @pl.when(2 * tile + core != me)
            def _():
                forward_copy(2 * tile + core, me, 0, 2).start()

        return carry

    lax.fori_loop(1, 9, gate_tile, 0)
    rim_copy(nxt).wait()
    lax.fori_loop(1, 9, gate_head, 0)
    own = pltpu.make_async_copy(
        send_v.at[me], recv_v.at[:, pl.ds(pl.multiple_of(me * 16, 16), 16), :], local_sem.at[0]
    )
    own.start()

    def first_stage(source, pair, carry):
        x = jnp.concatenate([source[2 * pair], source[2 * pair + 1]], axis=1)
        y = dot(first_v[...], x).astype(BF16)
        y_v[2 * pair] = y[:, :LANES]
        y_v[2 * pair + 1] = y[:, LANES:]
        return carry

    def second_stage(group):
        rows = y_v[:, pl.ds(pl.multiple_of(group * 16, 16), 16), :].reshape(256, LANES)
        return dot(second_v[group], rows)

    for load in loads[4:7]:
        load.wait()

    def filter_rows(block, carry):
        x = filt_v[:, pl.ds(pl.multiple_of(block * 256, 256), 256)].astype(BF16)
        x = jnp.concatenate([x, x], axis=0)
        x = lax.dot_general(perm_v[...], x, (((1,), (1,)), ((), ())), preferred_element_type=F32)
        x = x.astype(BF16).reshape(16, 16, LANES)
        fx_v[:, pl.ds(pl.multiple_of(block * 16, 16), 16), :] = x
        return carry

    def filter_group(group, carry):
        spec = second_stage(group)
        fs_v[group, :LANES] = spec[:LANES]
        fs_v[group, LANES:] = jnp.where(low_lanes(LANES), spec[LANES:], -spec[LANES:])
        return carry

    lax.fori_loop(0, 16, filter_rows, 0)
    lax.fori_loop(0, 8, functools.partial(first_stage, fx_v), 0)
    lax.fori_loop(0, GROUPS, filter_group, 0, unroll=UNROLL)
    for load in loads[7:]:
        load.wait()

    own.wait()

    whole_forward = pltpu.make_async_remote_copy(
        src_ref=send_v.at[pl.ds(0, 15)], dst_ref=recv_v.at[:, pl.ds(0, 240), :],
        send_sem=a_ss.at[0], recv_sem=a_rs.at[0], device_id={"ctx": nxt}, device_id_type=MESH,
    )
    whole_forward.wait_recv()

    lax.fori_loop(0, 8, functools.partial(first_stage, recv_v), 0, unroll=U1)

    def middle_group(group, carry):
        spec = second_stage(group)
        spec_v[group] = spec
        sr, si = spec[:LANES], spec[LANES:]
        fr, fi = fs_v[group, :LANES], fs_v[group, LANES:]
        freq = jnp.concatenate([sr * fr - si * fi, sr * fi + si * fr], axis=0).astype(BF16)
        back = dot(secondt_v[group], freq).astype(BF16).reshape(16, 16, LANES)
        z_v[:, pl.ds(pl.multiple_of(group * 16, 16), 16), :] = back
        return carry

    lax.fori_loop(0, GROUPS, middle_group, 0, unroll=U3)

    def last_stage(pair, carry):
        both = jnp.concatenate([z_v[2 * pair], z_v[2 * pair + 1]], axis=1)
        both = dot(firstt_v[...], both).astype(BF16)
        ysend_v[2 * pair] = both[:, :LANES]
        ysend_v[2 * pair + 1] = both[:, LANES:]
        return carry

    def back_copy(to, source, half):
        return pltpu.make_async_remote_copy(
            src_ref=ysend_v.at[pl.ds(half * 8, 8), pl.ds(pl.multiple_of(to * 16, 16), 16), :],
            dst_ref=brecv_v.at[source, pl.ds(half * 8, 8)],
            send_sem=b_ss.at[0], recv_sem=b_rs.at[source], device_id={"ctx": to}, device_id_type=MESH,
        )

    def whole_back(source):
        return pltpu.make_async_remote_copy(
            src_ref=ysend_v.at[:, pl.ds(0, 240), :], dst_ref=brecv_v.at[source],
            send_sem=b_ss.at[0], recv_sem=b_rs.at[source], device_id={"ctx": nxt}, device_id_type=MESH,
        )

    for half in range(2):
        lax.fori_loop(4 * half, 4 * half + 4, last_stage, 0, unroll=U2)

        def send_back(step, carry, half=half):
            back_copy(lax.rem(me + step, 16), me, half).start()
            return carry

        lax.fori_loop(1, 16, send_back, 0)

    own_back = pltpu.make_async_copy(
        ysend_v.at[:, pl.ds(pl.multiple_of(me * 16, 16), 16), :], brecv_v.at[me], local_sem.at[1]
    )
    own_back.start()
    def cross_group(group, carry):
        spec = spec_v[group]
        sr, si = spec[:LANES], spec[LANES:]
        rr, ri = pltpu.roll(sr, HALF, 1), pltpu.roll(si, HALF, 1)
        cross = ri * sr - rr * si
        cross = jnp.where(low_lanes(LANES), cross, -cross)
        freq = jnp.concatenate([sr * rr + si * ri, cross], axis=0).astype(BF16)
        back = dot(secondt_v[group], freq).astype(BF16).reshape(16, 16, LANES)
        y_v[:, pl.ds(pl.multiple_of(group * 16, 16), 16), :] = back
        return carry

    def cross_last(pair, carry):
        both = jnp.concatenate([y_v[2 * pair], y_v[2 * pair + 1]], axis=1)
        both = dot(firstt_v[...], both)
        grad = jnp.where(low_lanes(256), both[:, :LANES], both[:, LANES:]) * scale
        fsend_v[pair] = grad.astype(BF16)
        return carry

    lax.fori_loop(0, GROUPS, cross_group, 0, unroll=UNROLL)
    lax.fori_loop(0, 8, cross_last, 0)
    row_y, low_x = dpi // 2, lax.rem(dpi, 2)

    def filter_copy(to, source):
        return pltpu.make_async_remote_copy(
            src_ref=fsend_v.at[:, pl.ds(pl.multiple_of(to * 64, 64), 64), :], dst_ref=frecv_v.at[source],
            send_sem=f_ss.at[0], recv_sem=f_rs.at[0], device_id={"dp": 2 * to + low_x}, device_id_type=MESH,
        )

    for step in range(1, 4):
        filter_copy(lax.rem(row_y + step, 4), row_y).start()
    own_filter = pltpu.make_async_copy(
        fsend_v.at[:, pl.ds(pl.multiple_of(row_y * 64, 64), 64), :], frecv_v.at[row_y], local_sem.at[2]
    )
    own_filter.start()
    own_back.wait()
    own_filter.wait()
    whole_filter = pltpu.make_async_remote_copy(
        src_ref=fsend_v.at[:, pl.ds(0, 192), :], dst_ref=frecv_v.at[pl.ds(0, 3)],
        send_sem=f_ss.at[0], recv_sem=f_rs.at[0], device_id={"dp": dpi}, device_id_type=MESH,
    )
    half_filter = pltpu.make_async_remote_copy(
        src_ref=hsend_v, dst_ref=hrecv_v, send_sem=h_ss.at[0], recv_sem=h_rs.at[0],
        device_id={"dp": dpi + 1 - 2 * low_x}, device_id_type=MESH,
    )

    def filter_sum(pair, start):
        rows = pl.ds(pl.multiple_of(start, 32), 32)
        value = frecv_v[0, pair, rows, :].astype(F32)
        for at in range(1, 4):
            value = value + frecv_v[at, pair, rows, :].astype(F32)
        return value

    def filter_half(pair, carry):
        hsend_v[pair] = filter_sum(pair, 32 - 32 * low_x).astype(BF16)
        return carry

    def sum_copy(to, source):
        return pltpu.make_async_remote_copy(
            src_ref=asend_v.at[to], dst_ref=arecv_v.at[source], send_sem=s_ss.at[0], recv_sem=s_rs.at[0],
            device_id={"ctx": side * 8 + to}, device_id_type=MESH,
        )

    def partial(x):
        return jnp.sum(x.reshape(CHUNK // 8, 8, LANES), axis=0)

    def down(x):
        return jnp.sum(x, axis=0, keepdims=True)

    def ready_tile(tile, carry):
        cols = pl.ds(pl.multiple_of(tile * LANES, LANES), LANES)
        gain = skip_v[:, cols]
        total = jnp.zeros((8, LANES), F32)
        for top in range(0, 256, CHUNK):
            rows = pl.ds(top, CHUNK)
            queries, keys, values = (mix_v[part, rows, cols] for part in range(3))
            cot = cot_v[rows, cols].astype(F32)
            product = (keys * values).astype(BF16).astype(F32)
            grad = (cot * queries).astype(BF16).astype(F32)
            ready_v[0, rows, cols] = gain * product
            ready_v[1, rows, cols] = gain * grad
            ready_v[2, rows, cols] = cot
            total = total + partial(grad * product)
            for part in range(3):
                cut = pl.ds(pl.multiple_of(tile * LANES + part * 1024, LANES), LANES)
                one, two, _ = earlier(cut, top, rim_v[:, cut].astype(F32)[8:16] * keep)
                xs_v[0, rows, cut] = one
                xs_v[1, rows, cut] = two
        asend_v[tile, 9:10] = down(total)
        return carry

    lax.fori_loop(0, 8, ready_tile, 0)
    def grad_tile(step, carry):
        tile = lax.rem(side * 4 + step, 8)
        cols = pl.ds(pl.multiple_of(tile * LANES, LANES), LANES)
        for core in range(2):

            @pl.when(2 * tile + core != me)
            def _():
                whole_back(2 * tile + core).wait_recv()

        pair = jnp.concatenate(
            [brecv_v[2 * tile].reshape(256, LANES), brecv_v[2 * tile + 1].reshape(256, LANES)], axis=1
        )
        pair_v[...] = dot(unperm_v[...], pair)
        totals = [jnp.zeros((8, LANES), F32)] * 9
        low = low_lanes(CHUNK)
        for top in range(0, 256, CHUNK):
            rows = pl.ds(top, CHUNK)
            even, odd = pair_v[rows, :LANES], pair_v[rows, LANES:]
            gated = jnp.where(low, even, pltpu.roll(odd, HALF, 1)) + ready_v[0, rows, cols]
            product_grad = jnp.where(low, pltpu.roll(even, HALF, 1), odd) + ready_v[1, rows, cols]
            queries, keys, values = (mix_v[part, rows, cols] for part in range(3))
            out_v[rows, cols] = (queries * gated).astype(BF16)
            grads = (ready_v[2, rows, cols] * gated, product_grad * values, product_grad * keys)
            for part, mixed_grad in enumerate(grads):
                cut = pl.ds(pl.multiple_of(tile * LANES + part * 1024, LANES), LANES)
                rounded = mixed_grad.astype(BF16)
                mg_v[rows, cut] = rounded
                mg = rounded.astype(F32)
                if top == 0:
                    rsend_v[tile, 2 * part : 2 * part + 2] = mg[:2]
                lagged = (proj_v[rows, cut].astype(F32), xs_v[0, rows, cut], xs_v[1, rows, cut])
                for tap in range(3):
                    totals[3 * part + tap] = totals[3 * part + tap] + partial(mg * lagged[tap])
        for at in range(9):
            asend_v[tile, at : at + 1] = down(totals[at])

        @pl.when(tile != seat)
        def _():
            sum_copy(tile, seat).start()

        return carry

    rsend_v[...] = jnp.zeros_like(rsend_v)
    lax.fori_loop(0, 8, grad_tile, 0)
    rims = pltpu.make_async_remote_copy(
        src_ref=rsend_v, dst_ref=rrecv_v, send_sem=r_ss.at[0], recv_sem=r_rs.at[0],
        device_id={"ctx": prv}, device_id_type=MESH,
    )
    rims.start()
    arecv_v[seat] = asend_v[seat]
    whole_filter.wait_recv()
    lax.fori_loop(0, 8, filter_half, 0)
    half_filter.start()

    whole_sums = pltpu.make_async_remote_copy(
        src_ref=asend_v.at[pl.ds(0, 7)], dst_ref=arecv_v.at[pl.ds(0, 7)],
        send_sem=s_ss.at[0], recv_sem=s_rs.at[0], device_id={"ctx": nxt}, device_id_type=MESH,
    )
    whole_sums.wait_recv()
    total = arecv_v[0]
    for at in range(1, 8):
        total = total + arecv_v[at]
    dsend_v[0] = total
    drecv_v[line] = total

    def part_copy(to, source):
        return pltpu.make_async_remote_copy(
            src_ref=dsend_v.at[0], dst_ref=drecv_v.at[source], send_sem=d_ss.at[0], recv_sem=d_rs.at[0],
            device_id=line_id(to), device_id_type=MESH,
        )

    def all_copy(to, source):
        return pltpu.make_async_remote_copy(
            src_ref=gsend_v.at[0], dst_ref=grecv_v.at[source], send_sem=g_ss.at[0], recv_sem=g_rs.at[0],
            device_id={"ctx": side * 8 + to}, device_id_type=MESH,
        )

    for step in range(1, 16):
        part_copy(lax.rem(line + step, 16), line).start()

    keep_back = jnp.where(me == 15, 0.0, 1.0).astype(F32)
    rims.wait_recv()

    def last_tile(tile, carry):
        for part in range(3):
            cut = pl.ds(pl.multiple_of(tile * LANES + part * 1024, LANES), LANES)
            rim = pltpu.roll(rrecv_v[tile], 8 - 2 * part, 0) if part else rrecv_v[tile]
            rim = rim * keep_back
            w = short_v[:, cut]
            for top in range(0, 256, CHUNK):
                mg = mg_v[pl.ds(top, CHUNK), cut].astype(F32)
                after = mg_v[pl.ds(top + CHUNK, 16), cut].astype(F32)[:8] if top + CHUNK < 256 else rim
                value = w[0:1] * mg + w[1:2] * advanced(mg, after, 1) + w[2:3] * advanced(mg, after, 2)
                pg_v[pl.ds(top, CHUNK), cut] = value.astype(BF16)
        return carry

    lax.fori_loop(0, 4, last_tile, 0)

    whole_parts = pltpu.make_async_remote_copy(
        src_ref=dsend_v.at[pl.ds(0, 15)], dst_ref=drecv_v.at[pl.ds(0, 15)],
        send_sem=d_ss.at[0], recv_sem=d_rs.at[0], device_id={"ctx": nxt}, device_id_type=MESH,
    )
    whole_parts.wait_recv()
    total = drecv_v[0]
    for at in range(1, 16):
        total = total + drecv_v[at]
    total = total * scale
    gsend_v[0] = total
    grecv_v[seat] = total
    for step in range(1, 8):
        all_copy(lax.rem(seat + step, 8), seat).start()

    lax.fori_loop(4, 8, last_tile, 0)
    half_filter.wait_recv()
    for pair in range(8):
        value = filter_sum(pair, 32 * low_x) + hrecv_v[pair].astype(F32)
        wide_v[pl.ds(2 * pair, 32, 16), :] = value
        wide_v[pl.ds(2 * pair + 1, 32, 16), :] = pltpu.roll(value, HALF, 1)
    fg_v[...] = jnp.transpose(wide_v[...])[:HALF]
    whole_forward.wait_send()
    whole_back(me).wait_send()
    whole_filter.wait_send()
    half_filter.wait_send()
    rims.wait_send()
    whole_sums.wait_send()
    whole_parts.wait_send()
    whole_all = pltpu.make_async_remote_copy(
        src_ref=gsend_v.at[pl.ds(0, 7)], dst_ref=grecv_v.at[pl.ds(0, 7)],
        send_sem=g_ss.at[0], recv_sem=g_rs.at[0], device_id={"ctx": nxt}, device_id_type=MESH,
    )
    whole_all.wait_recv()
    whole_all.wait_send()


def result_kernel(out_v, pg_v, sums_v, fg_v, out_r, pg_r, sg_r, skg_r, fg_r, sg_v, skg_v, sem):
    copies = [
        pltpu.make_async_copy(src, dst, sem.at[at])
        for at, (src, dst) in enumerate([(pg_v, pg_r), (out_v, out_r), (fg_v, fg_r), (sg_v, sg_r), (skg_v, skg_r)])
    ]
    for copy in copies[:3]:
        copy.start()
    for tile in range(8):
        for at in range(9):
            part, tap = at // 3, at % 3
            left = part * 1024 + tile * LANES
            sg_v[tap : tap + 1, left : left + LANES] = sums_v[tile, at : at + 1]
        skg_v[:, tile * LANES : tile * LANES + LANES] = sums_v[tile, 9:10]
    for copy in copies[3:]:
        copy.start()
    for copy in copies:
        copy.wait()


def shards(proj, short_w, filt, skip_gain, cotangent):
    width = skip_gain.shape[0]
    scale = 1.0 / math.sqrt(proj.shape[0] * lax.axis_size("dp") * lax.axis_size("ctx"))
    whole = pl.BlockSpec(memory_space=pl.ANY)
    inside = pl.BlockSpec(memory_space=pltpu.VMEM)
    dma = pltpu.SemaphoreType.DMA
    outs = pl.pallas_call(
        functools.partial(kernel, scale),
        out_shape=[
            pltpu.VMEM((256, 1024), BF16),
            pltpu.VMEM((256, 3072), BF16),
            pltpu.VMEM((8, 16, LANES), F32),
            pltpu.VMEM((HALF, 512), F32),
        ],
        in_specs=[whole] * 11,
        out_specs=[inside] * 4,
        scratch_shapes=[
            pltpu.VMEM((256, 3072), BF16),
            pltpu.VMEM((256, 1024), BF16),
            pltpu.VMEM((HALF, 4096), F32),
            pltpu.VMEM((3, 3072), F32),
            pltpu.VMEM((1, 1024), F32),
            pltpu.VMEM((256, 256), BF16),
            pltpu.VMEM((256, 256), BF16),
            pltpu.VMEM((2 * HI, HI), BF16),
            pltpu.VMEM((GROUPS, 256, 256), BF16),
            pltpu.VMEM((HI, 2 * HI), BF16),
            pltpu.VMEM((GROUPS, 256, 256), BF16),
            pltpu.VMEM((16, 3072), BF16),
            pltpu.VMEM((3, 256, 1024), F32),
            pltpu.VMEM((16, 16, 16, LANES), BF16),
            pltpu.VMEM((LO, HI, LANES), BF16),
            pltpu.VMEM((LO, HI, LANES), BF16),
            pltpu.VMEM((LO, 2 * HI, LANES), BF16),
            pltpu.VMEM((GROUPS, 256, LANES), F32),
            pltpu.VMEM((GROUPS, 256, LANES), F32),
            pltpu.VMEM((LO, 2 * HI, LANES), BF16),
            pltpu.VMEM((LO, HI, LANES), BF16),
            pltpu.VMEM((16, LO, 16, LANES), BF16),
            pltpu.VMEM((8, HI, LANES), BF16),
            pltpu.VMEM((4, 8, 64, LANES), BF16),
            pltpu.VMEM((8, 32, LANES), BF16),
            pltpu.VMEM((8, 32, LANES), BF16),
            pltpu.VMEM((2, 256, 3072), F32),
            pltpu.VMEM((3, 256, 1024), F32),
            pltpu.VMEM((256, 3072), BF16),
            pltpu.VMEM((256, 2 * LANES), BF16),
            pltpu.VMEM((256, 2 * LANES), F32),
            pltpu.VMEM((8, 8, LANES), F32),
            pltpu.VMEM((8, 8, LANES), F32),
            pltpu.VMEM((8, 16, LANES), F32),
            pltpu.VMEM((8, 16, LANES), F32),
            pltpu.VMEM((16, 16, LANES), F32),
            pltpu.VMEM((16, 16, LANES), F32),
            pltpu.VMEM((8, 16, LANES), F32),
            pltpu.VMEM((512, LANES), F32),
            dma((11,)),
            dma((1,)), dma((1,)), dma((1,)), dma((1,)), dma((1,)), dma((16,)), dma((1,)), dma((1,)),
            dma((1,)), dma((1,)), dma((1,)), dma((1,)), dma((1,)), dma((1,)), dma((1,)), dma((1,)),
            dma((1,)), dma((1,)), dma((3,)),
        ],
        compiler_params=pltpu.CompilerParams(
            collective_id=0, has_side_effects=True, vmem_limit_bytes=56 * 1024 * 1024
        ),
    )(proj, cotangent, filt.T, short_w, skip_gain.reshape(1, width), *tables())
    outs = [pltpu.with_memory_space_constraint(value, pltpu.VMEM) for value in outs]
    outputs, proj_grad, short_grad, skip_grad, filt_grad = pl.pallas_call(
        result_kernel,
        out_shape=[
            jax.ShapeDtypeStruct((256, 1024), BF16),
            jax.ShapeDtypeStruct((256, 3072), BF16),
            jax.ShapeDtypeStruct((3, 3072), F32),
            jax.ShapeDtypeStruct((1, 1024), F32),
            jax.ShapeDtypeStruct((HALF, 512), F32),
        ],
        in_specs=[inside] * 4,
        out_specs=[whole] * 5,
        scratch_shapes=[pltpu.VMEM((3, 3072), F32), pltpu.VMEM((1, 1024), F32), dma((5,))],
    )(*outs)
    return (outputs, proj_grad, short_grad, skip_grad.reshape(width), filt_grad.T)


def solution(mesh):
    placed = (P(("dp", "ctx"), None), P(), P(None, "ctx"), P(), P(("dp", "ctx"), None))
    return jax.shard_map(
        shards,
        mesh=mesh,
        in_specs=placed,
        out_specs=(P(("dp", "ctx"), None), P(("dp", "ctx"), None), P(), P(), P("dp", "ctx")),
        check_vma=False,
    )
```

```python
import functools
import math

import jax
import jax.numpy as jnp
import ml_dtypes
import numpy as np
from jax import lax
from jax.experimental import pallas as pl
from jax.experimental.pallas import tpu as pltpu
from jax.sharding import PartitionSpec as P

HI = 256
LO = 16
GROUP = 8
GROUPS = HI // GROUP
UNROLL = 4
U1 = 8
PIECES = 4
U3 = 32
CHUNK = 32
LANES = 128
HALF = 64
MESH = pl.DeviceIdType.MESH
F32 = jnp.float32
BF16 = jnp.bfloat16


def tables():
    total = HI * LO
    start = np.arange(HI)
    angle = 2.0 * math.pi / HI * ((start[:, None] + 0.25) * np.arange(HI)[None, :] % HI)
    first = np.stack([np.cos(angle), -np.sin(angle)])
    first = first.reshape(2, GROUPS, GROUP, HI).transpose(1, 0, 2, 3).reshape(2 * HI, HI)
    freq = HI * np.arange(LO)[None, None, :] + start.reshape(GROUPS, GROUP)[:, :, None] + 0.25
    angle = 2.0 * math.pi / total * (freq[..., None] * np.arange(LO) % total)
    second = np.zeros((GROUPS, 2, LO, GROUP, LO, 2, GROUP))
    for at in range(GROUP):
        second[:, 0, :, at, :, 0, at] = np.cos(angle[:, at])
        second[:, 0, :, at, :, 1, at] = np.sin(angle[:, at])
        second[:, 1, :, at, :, 0, at] = -np.sin(angle[:, at])
        second[:, 1, :, at, :, 1, at] = np.cos(angle[:, at])
    second = second.reshape(GROUPS, 2 * LO * GROUP, 2 * LO * GROUP)
    rows = np.arange(256)
    perm = np.zeros((256, 256))
    perm[rows, rows % 16 * LO + rows // 16] = 1.0
    return [
        table.astype(ml_dtypes.bfloat16)
        for table in (perm, perm.T, first, second, first.T / total, second.transpose(0, 2, 1))
    ]


def dot(left, right):
    return jnp.dot(left, right, preferred_element_type=F32)


def low_lanes(rows):
    return lax.broadcasted_iota(jnp.int32, (rows, LANES), 1) < HALF


def delayed(x, rim, steps):
    turned = pltpu.roll(x, steps, 0)
    before = pltpu.roll(rim, steps, 0)
    row = lax.broadcasted_iota(jnp.int32, (8, LANES), 0)
    return jnp.concatenate([jnp.where(row < steps, before, turned[:8]), turned[8:]], axis=0)


def advanced(x, rim, steps):
    rows = x.shape[0]
    turned = pltpu.roll(x, rows - steps, 0)
    after = pltpu.roll(rim, 8 - steps, 0)
    row = lax.broadcasted_iota(jnp.int32, (8, LANES), 0)
    return jnp.concatenate(
        [turned[: rows - 8], jnp.where(row < 8 - steps, turned[rows - 8 :], after)], axis=0
    )


def kernel(
    scale,
    proj_h, cot_h, filt_h, short_h, skip_h, perm_h, unperm_h, first_h, second_h, firstt_h, secondt_h,
    out_v, pg_v, grecv_v, fg_v,
    proj_v, cot_v, filt_v, short_v, skip_v, perm_v, unperm_v, first_v, second_v, firstt_v, secondt_v,
    rim_v, mix_v, send_v, recv_v, fx_v, y_v, fs_v, spec_v, z_v, ysend_v, brecv_v, fsend_v, frecv_v, hsend_v, hrecv_v,
    xs_v, ready_v, mg_v, gates_v, pair_v, rsend_v, rrecv_v, asend_v, arecv_v, dsend_v, drecv_v, gsend_v, wide_v,
    load_sem, half_sem, rim_ss, rim_rs, a_ss, a_rs, b_ss, b_rs, f_ss, f_rs, h_ss, h_rs, r_ss, r_rs, s_ss, s_rs, d_ss, d_rs,
    g_ss, g_rs, local_sem,
):
    me = lax.axis_index("ctx")
    dpi = lax.axis_index("dp")
    side, seat = me // 8, lax.rem(me, 8)
    level = seat // 2
    nxt = lax.rem(me + 1, 16)
    prv = lax.rem(me + 15, 16)

    barrier = pltpu.get_barrier_semaphore()
    for step in range(1, 16):
        pl.semaphore_signal(
            barrier, inc=1, device_id={"ctx": lax.rem(me + step, 16)}, device_id_type=MESH
        )
    line = side * 8 + dpi

    def line_id(at):
        return {"dp": lax.rem(at, 8), "ctx": at // 8 * 8 + seat}

    for step in (1, 2, 3, 4, 5, 6, 7, 9, 10, 11, 12, 13, 14, 15):
        pl.semaphore_signal(
            barrier, inc=1, device_id=line_id((side if step < 8 else 1 - side) * 8 +
            lax.rem(dpi + step, 8)), device_id_type=MESH,
        )

    loads = [
        pltpu.make_async_copy(src, dst, load_sem.at[at])
        for at, (src, dst) in enumerate(
            [
                (short_h, short_v), (perm_h, perm_v), (filt_h, filt_v),
                (first_h, first_v), (second_h, second_v), (secondt_h, secondt_v), (firstt_h, firstt_v),
                (unperm_h, unperm_v), (skip_h, skip_v),
            ]
        )
    ]
    def half_loads(which):
        copies = []
        for part in range(4):
            cut = pl.ds(pl.multiple_of(which * 512 + part % 3 * 1024, 512), 512)
            src, dst = (proj_h, proj_v) if part < 3 else (cot_h, cot_v)
            copies.append(pltpu.make_async_copy(src.at[:, cut], dst.at[:, cut], half_sem.at[part, which]))
        return copies

    def half_wait(which):
        for copy in half_loads(which):
            copy.wait()

    for copy in half_loads(1 - side) + loads[:2] + half_loads(side):
        copy.start()
    asend_v[...] = jnp.zeros_like(asend_v)
    pl.semaphore_wait(barrier, 29)

    def rim_copy(to):
        return pltpu.make_async_remote_copy(
            src_ref=proj_h.at[pl.ds(240, 16), :], dst_ref=rim_v, send_sem=rim_ss.at[0], recv_sem=rim_rs.at[0],
            device_id={"ctx": to}, device_id_type=MESH,
        )

    rim_copy(nxt).start()
    half_wait(1 - side)
    for load in loads[:2]:
        load.wait()
    keep = jnp.where(me == 0, 0.0, 1.0).astype(F32)

    def forward_copy(to, source, start, count):
        return pltpu.make_async_remote_copy(
            src_ref=send_v.at[to, pl.ds(start, count)],
            dst_ref=recv_v.at[pl.ds(start, count), pl.ds(pl.multiple_of(source * 16, 16), 16), :],
            send_sem=a_ss.at[0], recv_sem=a_rs.at[0], device_id={"ctx": to}, device_id_type=MESH,
        )

    def earlier(cut, top, rim=None):
        x = proj_v[pl.ds(top, CHUNK), cut].astype(F32)
        before = proj_v[pl.ds(top - 16, 16), cut].astype(F32)[8:] if top else rim
        if before is None:
            before = jnp.zeros((8, LANES), F32)
        return delayed(x, before, 1), delayed(x, before, 2), x

    def far_first(step):
        across = 1 - step // 4
        return lax.rem(side + across, 2) * 4 + lax.rem(level + step + 1, 4)

    def gate_tile(step, carry):
        tile = far_first(step)
        cols = pl.ds(pl.multiple_of(tile * LANES, LANES), LANES)
        for top in range(0, 256, CHUNK):
            rows = pl.ds(top, CHUNK)
            mixed = []
            for part in range(3):
                cut = pl.ds(pl.multiple_of(tile * LANES + part * 1024, LANES), LANES)
                one, two, x = earlier(cut, top)
                w = short_v[:, cut]
                value = w[0:1] * x + w[1:2] * one + w[2:3] * two
                mix_v[part, rows, cols] = value
                mixed.append(value)
            gates_v[rows, :LANES] = (mixed[1] * mixed[2]).astype(BF16)
            gates_v[rows, LANES:] = (cot_v[rows, cols].astype(F32) * mixed[0]).astype(BF16)
        both = dot(perm_v[...], gates_v[...])
        p, g = both[:, :LANES], both[:, LANES:]
        low = low_lanes(256)
        even = jnp.where(low, p, pltpu.roll(g, HALF, 1))
        odd = jnp.where(low, pltpu.roll(p, HALF, 1), g)
        send_v[2 * tile] = even.astype(BF16).reshape(16, 16, LANES)
        send_v[2 * tile + 1] = odd.astype(BF16).reshape(16, 16, LANES)
        for core in range(2):

            @pl.when(2 * tile + core != me)
            def _():
                forward_copy(2 * tile + core, me, 2, 14).start()

        return carry

    def gate_head(step, carry):
        tile = far_first(step)
        cols = pl.ds(pl.multiple_of(tile * LANES, LANES), LANES)
        mixed = []
        for part in range(3):
            cut = pl.ds(pl.multiple_of(tile * LANES + part * 1024, LANES), LANES)
            x = proj_v[pl.ds(0, 16), cut].astype(F32)
            rim = rim_v[:, cut].astype(F32)[8:16] * keep
            w = short_v[:, cut]
            value = (w[0:1] * x + w[1:2] * delayed(x, rim, 1) + w[2:3] * delayed(x, rim, 2))[:8]
            mix_v[part, pl.ds(0, 8), cols] = value
            mixed.append(value)
        p = (mixed[1] * mixed[2]).astype(BF16).astype(F32)
        g = (cot_v[pl.ds(0, 16), cols].astype(F32)[:8] * mixed[0]).astype(BF16).astype(F32)
        low = low_lanes(8)
        row = lax.broadcasted_iota(jnp.int32, (16, LANES), 0)
        for core, head in enumerate(
            (jnp.where(low, p, pltpu.roll(g, HALF, 1)), jnp.where(low, pltpu.roll(p, HALF, 1), g))
        ):
            for at in range(2):
                block = send_v[2 * tile + core, at].astype(F32)
                block = jnp.where(row == 0, head[at : at + 1], block)
                send_v[2 * tile + core, at] = block.astype(BF16)

            @pl.when(2 * tile + core != me)
            def _():
                forward_copy(2 * tile + core, me, 0, 2).start()

        return carry

    lax.fori_loop(0, 4, gate_tile, 0)
    half_wait(side)
    lax.fori_loop(4, 8, gate_tile, 0)
    for load in loads[2:]:
        load.start()
    rim_copy(nxt).wait()
    lax.fori_loop(0, 8, gate_head, 0)
    own = pltpu.make_async_copy(
        send_v.at[me], recv_v.at[:, pl.ds(pl.multiple_of(me * 16, 16), 16), :], local_sem.at[0]
    )
    own.start()

    def first_stage(source, pair, carry):
        x = jnp.concatenate([source[2 * pair], source[2 * pair + 1]], axis=1)
        y = dot(first_v[...], x).astype(BF16)
        y_v[2 * pair] = y[:, :LANES]
        y_v[2 * pair + 1] = y[:, LANES:]
        return carry

    def second_stage(group):
        rows = y_v[:, pl.ds(pl.multiple_of(group * 16, 16), 16), :].reshape(256, LANES)
        return dot(second_v[group], rows)

    for load in loads[2:5]:
        load.wait()

    def filter_rows(block, carry):
        x = filt_v[:, pl.ds(pl.multiple_of(block * 256, 256), 256)].astype(BF16)
        x = jnp.concatenate([x, x], axis=0)
        x = lax.dot_general(perm_v[...], x, (((1,), (1,)), ((), ())), preferred_element_type=F32)
        x = x.astype(BF16).reshape(16, 16, LANES)
        fx_v[:, pl.ds(pl.multiple_of(block * 16, 16), 16), :] = x
        return carry

    def filter_group(group, carry):
        spec = second_stage(group)
        fs_v[group, :LANES] = spec[:LANES]
        fs_v[group, LANES:] = jnp.where(low_lanes(LANES), spec[LANES:], -spec[LANES:])
        return carry

    lax.fori_loop(0, 16, filter_rows, 0)
    lax.fori_loop(0, 8, functools.partial(first_stage, fx_v), 0)
    lax.fori_loop(0, GROUPS, filter_group, 0, unroll=UNROLL)
    for load in loads[5:]:
        load.wait()

    own.wait()

    whole_forward = pltpu.make_async_remote_copy(
        src_ref=send_v.at[pl.ds(0, 15)], dst_ref=recv_v.at[:, pl.ds(0, 240), :],
        send_sem=a_ss.at[0], recv_sem=a_rs.at[0], device_id={"ctx": nxt}, device_id_type=MESH,
    )
    whole_forward.wait_recv()

    lax.fori_loop(0, 8, functools.partial(first_stage, recv_v), 0, unroll=U1)

    def middle_group(group, carry):
        spec = second_stage(group)
        spec_v[group] = spec
        sr, si = spec[:LANES], spec[LANES:]
        fr, fi = fs_v[group, :LANES], fs_v[group, LANES:]
        freq = jnp.concatenate([sr * fr - si * fi, sr * fi + si * fr], axis=0).astype(BF16)
        back = dot(secondt_v[group], freq).astype(BF16).reshape(16, 16, LANES)
        z_v[:, pl.ds(pl.multiple_of(group * 16, 16), 16), :] = back
        return carry

    lax.fori_loop(0, GROUPS, middle_group, 0, unroll=U3)

    def last_stage(pair, carry):
        both = jnp.concatenate([z_v[2 * pair], z_v[2 * pair + 1]], axis=1)
        both = dot(firstt_v[...], both).astype(BF16)
        ysend_v[2 * pair] = both[:, :LANES]
        ysend_v[2 * pair + 1] = both[:, LANES:]
        return carry

    piece = LO // PIECES

    def back_copy(to, source, half):
        return pltpu.make_async_remote_copy(
            src_ref=ysend_v.at[pl.ds(half * piece, piece), pl.ds(pl.multiple_of(to * 16, 16), 16), :],
            dst_ref=brecv_v.at[source, pl.ds(half * piece, piece)],
            send_sem=b_ss.at[0], recv_sem=b_rs.at[source], device_id={"ctx": to}, device_id_type=MESH,
        )

    def whole_back(source):
        return pltpu.make_async_remote_copy(
            src_ref=ysend_v.at[:, pl.ds(0, 240), :], dst_ref=brecv_v.at[source],
            send_sem=b_ss.at[0], recv_sem=b_rs.at[source], device_id={"ctx": nxt}, device_id_type=MESH,
        )

    for half in range(PIECES):
        lax.fori_loop(8 // PIECES * half, 8 // PIECES * (half + 1), last_stage, 0, unroll=8 // PIECES)

        def send_back(step, carry, half=half):
            to = lax.rem(side + 1 - step // 8, 2) * 8 + lax.rem(seat + step + 1, 8)
            back_copy(to, me, half).start()
            return carry

        lax.fori_loop(0, 15, send_back, 0)

    own_back = pltpu.make_async_copy(
        ysend_v.at[:, pl.ds(pl.multiple_of(me * 16, 16), 16), :], brecv_v.at[me], local_sem.at[1]
    )
    own_back.start()
    def cross_group(group, carry):
        spec = spec_v[group]
        sr, si = spec[:LANES], spec[LANES:]
        rr, ri = pltpu.roll(sr, HALF, 1), pltpu.roll(si, HALF, 1)
        cross = ri * sr - rr * si
        cross = jnp.where(low_lanes(LANES), cross, -cross)
        freq = jnp.concatenate([sr * rr + si * ri, cross], axis=0).astype(BF16)
        back = dot(secondt_v[group], freq).astype(BF16).reshape(16, 16, LANES)
        y_v[:, pl.ds(pl.multiple_of(group * 16, 16), 16), :] = back
        return carry

    def cross_last(pair, carry):
        both = jnp.concatenate([y_v[2 * pair], y_v[2 * pair + 1]], axis=1)
        both = dot(firstt_v[...], both)
        grad = jnp.where(low_lanes(256), both[:, :LANES], both[:, LANES:]) * scale
        fsend_v[pair] = grad.astype(BF16)
        return carry

    lax.fori_loop(0, GROUPS, cross_group, 0, unroll=UNROLL)
    lax.fori_loop(0, 8, cross_last, 0)
    row_y, low_x = dpi // 2, lax.rem(dpi, 2)

    def filter_copy(to, source):
        return pltpu.make_async_remote_copy(
            src_ref=fsend_v.at[:, pl.ds(pl.multiple_of(to * 64, 64), 64), :], dst_ref=frecv_v.at[source],
            send_sem=f_ss.at[0], recv_sem=f_rs.at[0], device_id={"dp": 2 * to + low_x}, device_id_type=MESH,
        )

    for step in range(1, 4):
        filter_copy(lax.rem(row_y + step, 4), row_y).start()
    own_filter = pltpu.make_async_copy(
        fsend_v.at[:, pl.ds(pl.multiple_of(row_y * 64, 64), 64), :], frecv_v.at[row_y], local_sem.at[2]
    )
    own_filter.start()
    own_back.wait()
    own_filter.wait()
    whole_filter = pltpu.make_async_remote_copy(
        src_ref=fsend_v.at[:, pl.ds(0, 192), :], dst_ref=frecv_v.at[pl.ds(0, 3)],
        send_sem=f_ss.at[0], recv_sem=f_rs.at[0], device_id={"dp": dpi}, device_id_type=MESH,
    )
    half_filter = pltpu.make_async_remote_copy(
        src_ref=hsend_v, dst_ref=hrecv_v, send_sem=h_ss.at[0], recv_sem=h_rs.at[0],
        device_id={"dp": dpi + 1 - 2 * low_x}, device_id_type=MESH,
    )

    def filter_sum(pair, start):
        rows = pl.ds(pl.multiple_of(start, 32), 32)
        value = frecv_v[0, pair, rows, :].astype(F32)
        for at in range(1, 4):
            value = value + frecv_v[at, pair, rows, :].astype(F32)
        return value

    def filter_half(pair, carry):
        hsend_v[pair] = filter_sum(pair, 32 - 32 * low_x).astype(BF16)
        return carry

    def sum_copy(to, source):
        return pltpu.make_async_remote_copy(
            src_ref=asend_v.at[to], dst_ref=arecv_v.at[source], send_sem=s_ss.at[0], recv_sem=s_rs.at[0],
            device_id={"ctx": side * 8 + to}, device_id_type=MESH,
        )

    def partial(x):
        return jnp.sum(x.reshape(CHUNK // 8, 8, LANES), axis=0)

    def down(x):
        return jnp.sum(x, axis=0, keepdims=True)

    def ready_tile(tile, carry):
        cols = pl.ds(pl.multiple_of(tile * LANES, LANES), LANES)
        gain = skip_v[:, cols]
        total = jnp.zeros((8, LANES), F32)
        for top in range(0, 256, CHUNK):
            rows = pl.ds(top, CHUNK)
            queries, keys, values = (mix_v[part, rows, cols] for part in range(3))
            cot = cot_v[rows, cols].astype(F32)
            product = (keys * values).astype(BF16).astype(F32)
            grad = (cot * queries).astype(BF16).astype(F32)
            ready_v[0, rows, cols] = gain * product
            ready_v[1, rows, cols] = gain * grad
            ready_v[2, rows, cols] = cot
            total = total + partial(grad * product)
            for part in range(3):
                cut = pl.ds(pl.multiple_of(tile * LANES + part * 1024, LANES), LANES)
                one, two, _ = earlier(cut, top, rim_v[:, cut].astype(F32)[8:16] * keep)
                xs_v[0, rows, cut] = one
                xs_v[1, rows, cut] = two
        asend_v[tile, 9:10] = down(total)
        return carry

    lax.fori_loop(0, 8, ready_tile, 0)
    def grad_tile(step, carry):
        tile = lax.rem(side * 4 + step, 8)
        cols = pl.ds(pl.multiple_of(tile * LANES, LANES), LANES)
        for core in range(2):

            @pl.when(2 * tile + core != me)
            def _():
                whole_back(2 * tile + core).wait_recv()

        pair = jnp.concatenate(
            [brecv_v[2 * tile].reshape(256, LANES), brecv_v[2 * tile + 1].reshape(256, LANES)], axis=1
        )
        pair_v[...] = dot(unperm_v[...], pair)
        totals = [jnp.zeros((8, LANES), F32)] * 9
        low = low_lanes(CHUNK)
        for top in range(0, 256, CHUNK):
            rows = pl.ds(top, CHUNK)
            even, odd = pair_v[rows, :LANES], pair_v[rows, LANES:]
            gated = jnp.where(low, even, pltpu.roll(odd, HALF, 1)) + ready_v[0, rows, cols]
            product_grad = jnp.where(low, pltpu.roll(even, HALF, 1), odd) + ready_v[1, rows, cols]
            queries, keys, values = (mix_v[part, rows, cols] for part in range(3))
            out_v[rows, cols] = (queries * gated).astype(BF16)
            grads = (ready_v[2, rows, cols] * gated, product_grad * values, product_grad * keys)
            for part, mixed_grad in enumerate(grads):
                cut = pl.ds(pl.multiple_of(tile * LANES + part * 1024, LANES), LANES)
                rounded = mixed_grad.astype(BF16)
                mg_v[rows, cut] = rounded
                mg = rounded.astype(F32)
                if top == 0:
                    rsend_v[tile, 2 * part : 2 * part + 2] = mg[:2]
                lagged = (proj_v[rows, cut].astype(F32), xs_v[0, rows, cut], xs_v[1, rows, cut])
                for tap in range(3):
                    totals[3 * part + tap] = totals[3 * part + tap] + partial(mg * lagged[tap])
        for at in range(9):
            asend_v[tile, at : at + 1] = down(totals[at])

        @pl.when(tile != seat)
        def _():
            sum_copy(tile, seat).start()

        return carry

    rsend_v[...] = jnp.zeros_like(rsend_v)
    lax.fori_loop(0, 8, grad_tile, 0)
    rims = pltpu.make_async_remote_copy(
        src_ref=rsend_v, dst_ref=rrecv_v, send_sem=r_ss.at[0], recv_sem=r_rs.at[0],
        device_id={"ctx": prv}, device_id_type=MESH,
    )
    rims.start()
    arecv_v[seat] = asend_v[seat]
    whole_filter.wait_recv()
    lax.fori_loop(0, 8, filter_half, 0)
    half_filter.start()

    whole_sums = pltpu.make_async_remote_copy(
        src_ref=asend_v.at[pl.ds(0, 7)], dst_ref=arecv_v.at[pl.ds(0, 7)],
        send_sem=s_ss.at[0], recv_sem=s_rs.at[0], device_id={"ctx": nxt}, device_id_type=MESH,
    )
    whole_sums.wait_recv()
    total = arecv_v[0]
    for at in range(1, 8):
        total = total + arecv_v[at]
    dsend_v[0] = total
    drecv_v[line] = total

    def part_copy(to, source):
        return pltpu.make_async_remote_copy(
            src_ref=dsend_v.at[0], dst_ref=drecv_v.at[source], send_sem=d_ss.at[0], recv_sem=d_rs.at[0],
            device_id=line_id(to), device_id_type=MESH,
        )

    def all_copy(to, source):
        return pltpu.make_async_remote_copy(
            src_ref=gsend_v.at[0], dst_ref=grecv_v.at[source], send_sem=g_ss.at[0], recv_sem=g_rs.at[0],
            device_id={"ctx": side * 8 + to}, device_id_type=MESH,
        )

    for step in range(1, 16):
        part_copy(lax.rem(line + step, 16), line).start()

    keep_back = jnp.where(me == 15, 0.0, 1.0).astype(F32)
    rims.wait_recv()

    def last_tile(tile, carry):
        for part in range(3):
            cut = pl.ds(pl.multiple_of(tile * LANES + part * 1024, LANES), LANES)
            rim = pltpu.roll(rrecv_v[tile], 8 - 2 * part, 0) if part else rrecv_v[tile]
            rim = rim * keep_back
            w = short_v[:, cut]
            for top in range(0, 256, CHUNK):
                mg = mg_v[pl.ds(top, CHUNK), cut].astype(F32)
                after = mg_v[pl.ds(top + CHUNK, 16), cut].astype(F32)[:8] if top + CHUNK < 256 else rim
                value = w[0:1] * mg + w[1:2] * advanced(mg, after, 1) + w[2:3] * advanced(mg, after, 2)
                pg_v[pl.ds(top, CHUNK), cut] = value.astype(BF16)
        return carry

    lax.fori_loop(0, 4, last_tile, 0)

    whole_parts = pltpu.make_async_remote_copy(
        src_ref=dsend_v.at[pl.ds(0, 15)], dst_ref=drecv_v.at[pl.ds(0, 15)],
        send_sem=d_ss.at[0], recv_sem=d_rs.at[0], device_id={"ctx": nxt}, device_id_type=MESH,
    )
    whole_parts.wait_recv()
    total = drecv_v[0]
    for at in range(1, 16):
        total = total + drecv_v[at]
    total = total * scale
    gsend_v[0] = total
    grecv_v[seat] = total
    for step in range(1, 8):
        all_copy(lax.rem(seat + step, 8), seat).start()

    lax.fori_loop(4, 8, last_tile, 0)
    half_filter.wait_recv()
    for pair in range(8):
        value = filter_sum(pair, 32 * low_x) + hrecv_v[pair].astype(F32)
        wide_v[pl.ds(2 * pair, 32, 16), :] = value
        wide_v[pl.ds(2 * pair + 1, 32, 16), :] = pltpu.roll(value, HALF, 1)
    fg_v[...] = jnp.transpose(wide_v[...])[:HALF]
    whole_forward.wait_send()
    whole_back(me).wait_send()
    whole_filter.wait_send()
    half_filter.wait_send()
    rims.wait_send()
    whole_sums.wait_send()
    whole_parts.wait_send()
    whole_all = pltpu.make_async_remote_copy(
        src_ref=gsend_v.at[pl.ds(0, 7)], dst_ref=grecv_v.at[pl.ds(0, 7)],
        send_sem=g_ss.at[0], recv_sem=g_rs.at[0], device_id={"ctx": nxt}, device_id_type=MESH,
    )
    whole_all.wait_recv()
    whole_all.wait_send()


def result_kernel(out_v, pg_v, sums_v, fg_v, out_r, pg_r, sg_r, skg_r, fg_r, sg_v, skg_v, sem):
    copies = [
        pltpu.make_async_copy(src, dst, sem.at[at])
        for at, (src, dst) in enumerate([(pg_v, pg_r), (out_v, out_r), (fg_v, fg_r), (sg_v, sg_r), (skg_v, skg_r)])
    ]
    for copy in copies[:3]:
        copy.start()
    for tile in range(8):
        for at in range(9):
            part, tap = at // 3, at % 3
            left = part * 1024 + tile * LANES
            sg_v[tap : tap + 1, left : left + LANES] = sums_v[tile, at : at + 1]
        skg_v[:, tile * LANES : tile * LANES + LANES] = sums_v[tile, 9:10]
    for copy in copies[3:]:
        copy.start()
    for copy in copies:
        copy.wait()


def shards(proj, short_w, filt, skip_gain, cotangent):
    width = skip_gain.shape[0]
    scale = 1.0 / math.sqrt(proj.shape[0] * lax.axis_size("dp") * lax.axis_size("ctx"))
    whole = pl.BlockSpec(memory_space=pl.ANY)
    inside = pl.BlockSpec(memory_space=pltpu.VMEM)
    dma = pltpu.SemaphoreType.DMA
    outs = pl.pallas_call(
        functools.partial(kernel, scale),
        out_shape=[
            pltpu.VMEM((256, 1024), BF16),
            pltpu.VMEM((256, 3072), BF16),
            pltpu.VMEM((8, 16, LANES), F32),
            pltpu.VMEM((HALF, 512), F32),
        ],
        in_specs=[whole] * 11,
        out_specs=[inside] * 4,
        scratch_shapes=[
            pltpu.VMEM((256, 3072), BF16),
            pltpu.VMEM((256, 1024), BF16),
            pltpu.VMEM((HALF, 4096), F32),
            pltpu.VMEM((3, 3072), F32),
            pltpu.VMEM((1, 1024), F32),
            pltpu.VMEM((256, 256), BF16),
            pltpu.VMEM((256, 256), BF16),
            pltpu.VMEM((2 * HI, HI), BF16),
            pltpu.VMEM((GROUPS, 256, 256), BF16),
            pltpu.VMEM((HI, 2 * HI), BF16),
            pltpu.VMEM((GROUPS, 256, 256), BF16),
            pltpu.VMEM((16, 3072), BF16),
            pltpu.VMEM((3, 256, 1024), F32),
            pltpu.VMEM((16, 16, 16, LANES), BF16),
            pltpu.VMEM((LO, HI, LANES), BF16),
            pltpu.VMEM((LO, HI, LANES), BF16),
            pltpu.VMEM((LO, 2 * HI, LANES), BF16),
            pltpu.VMEM((GROUPS, 256, LANES), F32),
            pltpu.VMEM((GROUPS, 256, LANES), F32),
            pltpu.VMEM((LO, 2 * HI, LANES), BF16),
            pltpu.VMEM((LO, HI, LANES), BF16),
            pltpu.VMEM((16, LO, 16, LANES), BF16),
            pltpu.VMEM((8, HI, LANES), BF16),
            pltpu.VMEM((4, 8, 64, LANES), BF16),
            pltpu.VMEM((8, 32, LANES), BF16),
            pltpu.VMEM((8, 32, LANES), BF16),
            pltpu.VMEM((2, 256, 3072), F32),
            pltpu.VMEM((3, 256, 1024), F32),
            pltpu.VMEM((256, 3072), BF16),
            pltpu.VMEM((256, 2 * LANES), BF16),
            pltpu.VMEM((256, 2 * LANES), F32),
            pltpu.VMEM((8, 8, LANES), F32),
            pltpu.VMEM((8, 8, LANES), F32),
            pltpu.VMEM((8, 16, LANES), F32),
            pltpu.VMEM((8, 16, LANES), F32),
            pltpu.VMEM((16, 16, LANES), F32),
            pltpu.VMEM((16, 16, LANES), F32),
            pltpu.VMEM((8, 16, LANES), F32),
            pltpu.VMEM((512, LANES), F32),
            dma((9,)), dma((4, 2)),
            dma((1,)), dma((1,)), dma((1,)), dma((1,)), dma((1,)), dma((16,)), dma((1,)), dma((1,)),
            dma((1,)), dma((1,)), dma((1,)), dma((1,)), dma((1,)), dma((1,)), dma((1,)), dma((1,)),
            dma((1,)), dma((1,)), dma((3,)),
        ],
        compiler_params=pltpu.CompilerParams(
            collective_id=0, has_side_effects=True, vmem_limit_bytes=56 * 1024 * 1024
        ),
    )(proj, cotangent, filt.T, short_w, skip_gain.reshape(1, width), *tables())
    outs = [pltpu.with_memory_space_constraint(value, pltpu.VMEM) for value in outs]
    outputs, proj_grad, short_grad, skip_grad, filt_grad = pl.pallas_call(
        result_kernel,
        out_shape=[
            jax.ShapeDtypeStruct((256, 1024), BF16),
            jax.ShapeDtypeStruct((256, 3072), BF16),
            jax.ShapeDtypeStruct((3, 3072), F32),
            jax.ShapeDtypeStruct((1, 1024), F32),
            jax.ShapeDtypeStruct((HALF, 512), F32),
        ],
        in_specs=[inside] * 4,
        out_specs=[whole] * 5,
        scratch_shapes=[pltpu.VMEM((3, 3072), F32), pltpu.VMEM((1, 1024), F32), dma((5,))],
    )(*outs)
    return (outputs, proj_grad, short_grad, skip_grad.reshape(width), filt_grad.T)


def solution(mesh):
    placed = (P(("dp", "ctx"), None), P(), P(None, "ctx"), P(), P(("dp", "ctx"), None))
    return jax.shard_map(
        shards,
        mesh=mesh,
        in_specs=placed,
        out_specs=(P(("dp", "ctx"), None), P(("dp", "ctx"), None), P(), P(), P("dp", "ctx")),
        check_vma=False,
    )
```

```python
import functools
import math

import jax
import jax.numpy as jnp
import ml_dtypes
import numpy as np
from jax import lax
from jax.experimental import pallas as pl
from jax.experimental.pallas import tpu as pltpu
from jax.sharding import PartitionSpec as P

HI = 256
LO = 16
GROUP = 8
GROUPS = HI // GROUP
UNROLL = 4
U1 = 8
PIECES = 4
U3 = 32
CHUNK = 32
LANES = 128
HALF = 64
MESH = pl.DeviceIdType.MESH
F32 = jnp.float32
BF16 = jnp.bfloat16


def tables():
    total = HI * LO
    start = np.arange(HI)
    angle = 2.0 * math.pi / HI * ((start[:, None] + 0.25) * np.arange(HI)[None, :] % HI)
    first = np.stack([np.cos(angle), -np.sin(angle)])
    first = first.reshape(2, GROUPS, GROUP, HI).transpose(1, 0, 2, 3).reshape(2 * HI, HI)
    freq = HI * np.arange(LO)[None, None, :] + start.reshape(GROUPS, GROUP)[:, :, None] + 0.25
    angle = 2.0 * math.pi / total * (freq[..., None] * np.arange(LO) % total)
    second = np.zeros((GROUPS, 2, LO, GROUP, LO, 2, GROUP))
    for at in range(GROUP):
        second[:, 0, :, at, :, 0, at] = np.cos(angle[:, at])
        second[:, 0, :, at, :, 1, at] = np.sin(angle[:, at])
        second[:, 1, :, at, :, 0, at] = -np.sin(angle[:, at])
        second[:, 1, :, at, :, 1, at] = np.cos(angle[:, at])
    second = second.reshape(GROUPS, 2 * LO * GROUP, 2 * LO * GROUP)
    rows = np.arange(256)
    perm = np.zeros((256, 256))
    perm[rows, rows % 16 * LO + rows // 16] = 1.0
    return [
        table.astype(ml_dtypes.bfloat16)
        for table in (perm, perm.T, first, second, first.T / total, second.transpose(0, 2, 1))
    ]


def dot(left, right):
    return jnp.dot(left, right, preferred_element_type=F32)


def low_lanes(rows):
    return lax.broadcasted_iota(jnp.int32, (rows, LANES), 1) < HALF


def delayed(x, rim, steps):
    turned = pltpu.roll(x, steps, 0)
    before = pltpu.roll(rim, steps, 0)
    row = lax.broadcasted_iota(jnp.int32, (8, LANES), 0)
    return jnp.concatenate([jnp.where(row < steps, before, turned[:8]), turned[8:]], axis=0)


def advanced(x, rim, steps):
    rows = x.shape[0]
    turned = pltpu.roll(x, rows - steps, 0)
    after = pltpu.roll(rim, 8 - steps, 0)
    row = lax.broadcasted_iota(jnp.int32, (8, LANES), 0)
    return jnp.concatenate(
        [turned[: rows - 8], jnp.where(row < 8 - steps, turned[rows - 8 :], after)], axis=0
    )


def kernel(
    scale,
    proj_h, cot_h, filt_h, short_h, skip_h, perm_h, unperm_h, first_h, second_h, firstt_h, secondt_h,
    out_v, pg_v, grecv_v, fg_v,
    proj_v, cot_v, filt_v, short_v, skip_v, perm_v, unperm_v, first_v, second_v, firstt_v, secondt_v,
    rim_v, mix_v, send_v, recv_v, fx_v, y_v, fs_v, spec_v, z_v, ysend_v, brecv_v, fsend_v, frecv_v, hsend_v, hrecv_v,
    xs_v, ready_v, mg_v, gates_v, pair_v, rsend_v, rrecv_v, asend_v, arecv_v, dsend_v, drecv_v, gsend_v, wide_v,
    load_sem, half_sem, rim_ss, rim_rs, a_ss, a_rs, b_ss, b_rs, f_ss, f_rs, h_ss, h_rs, r_ss, r_rs, s_ss, s_rs, d_ss, d_rs,
    g_ss, g_rs, local_sem,
):
    me = lax.axis_index("ctx")
    dpi = lax.axis_index("dp")
    side, seat = me // 8, lax.rem(me, 8)
    level = seat // 2
    nxt = lax.rem(me + 1, 16)
    prv = lax.rem(me + 15, 16)

    barrier = pltpu.get_barrier_semaphore()
    for step in range(1, 16):
        pl.semaphore_signal(
            barrier, inc=1, device_id={"ctx": lax.rem(me + step, 16)}, device_id_type=MESH
        )
    line = side * 8 + dpi

    def line_id(at):
        return {"dp": lax.rem(at, 8), "ctx": at // 8 * 8 + seat}

    for step in (1, 2, 3, 4, 5, 6, 7, 9, 10, 11, 12, 13, 14, 15):
        pl.semaphore_signal(
            barrier, inc=1, device_id=line_id((side if step < 8 else 1 - side) * 8 +
            lax.rem(dpi + step, 8)), device_id_type=MESH,
        )

    loads = [
        pltpu.make_async_copy(src, dst, load_sem.at[at])
        for at, (src, dst) in enumerate(
            [
                (short_h, short_v), (perm_h, perm_v), (filt_h, filt_v),
                (first_h, first_v), (second_h, second_v), (secondt_h, secondt_v), (firstt_h, firstt_v),
                (unperm_h, unperm_v), (skip_h, skip_v),
            ]
        )
    ]
    def half_loads(which):
        copies = []
        for part in range(4):
            cut = pl.ds(pl.multiple_of(which * 512 + part % 3 * 1024, 512), 512)
            src, dst = (proj_h, proj_v) if part < 3 else (cot_h, cot_v)
            copies.append(pltpu.make_async_copy(src.at[:, cut], dst.at[:, cut], half_sem.at[part, which]))
        return copies

    def half_wait(which):
        for copy in half_loads(which):
            copy.wait()

    for copy in half_loads(1 - side) + loads[:2] + half_loads(side):
        copy.start()
    asend_v[...] = jnp.zeros_like(asend_v)
    pl.semaphore_wait(barrier, 29)

    def rim_copy(to):
        return pltpu.make_async_remote_copy(
            src_ref=proj_h.at[pl.ds(240, 16), :], dst_ref=rim_v, send_sem=rim_ss.at[0], recv_sem=rim_rs.at[0],
            device_id={"ctx": to}, device_id_type=MESH,
        )

    rim_copy(nxt).start()
    half_wait(1 - side)
    for load in loads[:2]:
        load.wait()
    keep = jnp.where(me == 0, 0.0, 1.0).astype(F32)

    def forward_copy(to, source, start, count):
        return pltpu.make_async_remote_copy(
            src_ref=send_v.at[to, pl.ds(start, count)],
            dst_ref=recv_v.at[pl.ds(start, count), pl.ds(pl.multiple_of(source * 16, 16), 16), :],
            send_sem=a_ss.at[0], recv_sem=a_rs.at[0], device_id={"ctx": to}, device_id_type=MESH,
        )

    def earlier(cut, top, rim=None):
        x = proj_v[pl.ds(top, CHUNK), cut].astype(F32)
        before = proj_v[pl.ds(top - 16, 16), cut].astype(F32)[8:] if top else rim
        if before is None:
            before = jnp.zeros((8, LANES), F32)
        return delayed(x, before, 1), delayed(x, before, 2), x

    def far_first(step):
        across = 1 - step // 4
        return lax.rem(side + across, 2) * 4 + lax.rem(level + step + 1, 4)

    def gate_tile(step, carry):
        tile = far_first(step)
        cols = pl.ds(pl.multiple_of(tile * LANES, LANES), LANES)
        for top in range(0, 256, CHUNK):
            rows = pl.ds(top, CHUNK)
            mixed = []
            for part in range(3):
                cut = pl.ds(pl.multiple_of(tile * LANES + part * 1024, LANES), LANES)
                one, two, x = earlier(cut, top)
                w = short_v[:, cut]
                value = w[0:1] * x + w[1:2] * one + w[2:3] * two
                mix_v[part, rows, cols] = value
                mixed.append(value)
            gates_v[rows, :LANES] = (mixed[1] * mixed[2]).astype(BF16)
            gates_v[rows, LANES:] = (cot_v[rows, cols].astype(F32) * mixed[0]).astype(BF16)
        both = dot(perm_v[...], gates_v[...])
        p, g = both[:, :LANES], both[:, LANES:]
        low = low_lanes(256)
        even = jnp.where(low, p, pltpu.roll(g, HALF, 1))
        odd = jnp.where(low, pltpu.roll(p, HALF, 1), g)
        send_v[2 * tile] = even.astype(BF16).reshape(16, 16, LANES)
        send_v[2 * tile + 1] = odd.astype(BF16).reshape(16, 16, LANES)
        for core in range(2):

            @pl.when(2 * tile + core != me)
            def _():
                forward_copy(2 * tile + core, me, 2, 14).start()

        return carry

    def gate_head(step, carry):
        tile = far_first(step)
        cols = pl.ds(pl.multiple_of(tile * LANES, LANES), LANES)
        mixed = []
        for part in range(3):
            cut = pl.ds(pl.multiple_of(tile * LANES + part * 1024, LANES), LANES)
            x = proj_v[pl.ds(0, 16), cut].astype(F32)
            rim = rim_v[:, cut].astype(F32)[8:16] * keep
            w = short_v[:, cut]
            value = (w[0:1] * x + w[1:2] * delayed(x, rim, 1) + w[2:3] * delayed(x, rim, 2))[:8]
            mix_v[part, pl.ds(0, 8), cols] = value
            mixed.append(value)
        p = (mixed[1] * mixed[2]).astype(BF16).astype(F32)
        g = (cot_v[pl.ds(0, 16), cols].astype(F32)[:8] * mixed[0]).astype(BF16).astype(F32)
        low = low_lanes(8)
        row = lax.broadcasted_iota(jnp.int32, (16, LANES), 0)
        for core, head in enumerate(
            (jnp.where(low, p, pltpu.roll(g, HALF, 1)), jnp.where(low, pltpu.roll(p, HALF, 1), g))
        ):
            for at in range(2):
                block = send_v[2 * tile + core, at].astype(F32)
                block = jnp.where(row == 0, head[at : at + 1], block)
                send_v[2 * tile + core, at] = block.astype(BF16)

            @pl.when(2 * tile + core != me)
            def _():
                forward_copy(2 * tile + core, me, 0, 2).start()

        return carry

    lax.fori_loop(0, 4, gate_tile, 0, unroll=2)
    half_wait(side)
    lax.fori_loop(4, 8, gate_tile, 0)
    for load in loads[2:]:
        load.start()
    rim_copy(nxt).wait()
    lax.fori_loop(0, 8, gate_head, 0)
    own = pltpu.make_async_copy(
        send_v.at[me], recv_v.at[:, pl.ds(pl.multiple_of(me * 16, 16), 16), :], local_sem.at[0]
    )
    own.start()

    def first_stage(source, pair, carry):
        x = jnp.concatenate([source[2 * pair], source[2 * pair + 1]], axis=1)
        y = dot(first_v[...], x).astype(BF16)
        y_v[2 * pair] = y[:, :LANES]
        y_v[2 * pair + 1] = y[:, LANES:]
        return carry

    def second_stage(group):
        rows = y_v[:, pl.ds(pl.multiple_of(group * 16, 16), 16), :].reshape(256, LANES)
        return dot(second_v[group], rows)

    for load in loads[2:5]:
        load.wait()

    def filter_rows(block, carry):
        x = filt_v[:, pl.ds(pl.multiple_of(block * 256, 256), 256)].astype(BF16)
        x = jnp.concatenate([x, x], axis=0)
        x = lax.dot_general(perm_v[...], x, (((1,), (1,)), ((), ())), preferred_element_type=F32)
        x = x.astype(BF16).reshape(16, 16, LANES)
        fx_v[:, pl.ds(pl.multiple_of(block * 16, 16), 16), :] = x
        return carry

    def filter_group(group, carry):
        spec = second_stage(group)
        fs_v[group, :LANES] = spec[:LANES]
        fs_v[group, LANES:] = jnp.where(low_lanes(LANES), spec[LANES:], -spec[LANES:])
        return carry

    lax.fori_loop(0, 16, filter_rows, 0)
    lax.fori_loop(0, 8, functools.partial(first_stage, fx_v), 0)
    lax.fori_loop(0, GROUPS, filter_group, 0, unroll=UNROLL)
    for load in loads[5:]:
        load.wait()

    own.wait()

    whole_forward = pltpu.make_async_remote_copy(
        src_ref=send_v.at[pl.ds(0, 15)], dst_ref=recv_v.at[:, pl.ds(0, 240), :],
        send_sem=a_ss.at[0], recv_sem=a_rs.at[0], device_id={"ctx": nxt}, device_id_type=MESH,
    )
    whole_forward.wait_recv()

    lax.fori_loop(0, 8, functools.partial(first_stage, recv_v), 0, unroll=U1)

    def middle_group(group, carry):
        spec = second_stage(group)
        spec_v[group] = spec
        sr, si = spec[:LANES], spec[LANES:]
        fr, fi = fs_v[group, :LANES], fs_v[group, LANES:]
        freq = jnp.concatenate([sr * fr - si * fi, sr * fi + si * fr], axis=0).astype(BF16)
        back = dot(secondt_v[group], freq).astype(BF16).reshape(16, 16, LANES)
        z_v[:, pl.ds(pl.multiple_of(group * 16, 16), 16), :] = back
        return carry

    lax.fori_loop(0, GROUPS, middle_group, 0, unroll=U3)

    def last_stage(pair, carry):
        both = jnp.concatenate([z_v[2 * pair], z_v[2 * pair + 1]], axis=1)
        both = dot(firstt_v[...], both).astype(BF16)
        ysend_v[2 * pair] = both[:, :LANES]
        ysend_v[2 * pair + 1] = both[:, LANES:]
        return carry

    piece = LO // PIECES

    def back_copy(to, source, half):
        return pltpu.make_async_remote_copy(
            src_ref=ysend_v.at[pl.ds(half * piece, piece), pl.ds(pl.multiple_of(to * 16, 16), 16), :],
            dst_ref=brecv_v.at[source, pl.ds(half * piece, piece)],
            send_sem=b_ss.at[0], recv_sem=b_rs.at[source], device_id={"ctx": to}, device_id_type=MESH,
        )

    def whole_back(source):
        return pltpu.make_async_remote_copy(
            src_ref=ysend_v.at[:, pl.ds(0, 240), :], dst_ref=brecv_v.at[source],
            send_sem=b_ss.at[0], recv_sem=b_rs.at[source], device_id={"ctx": nxt}, device_id_type=MESH,
        )

    for half in range(PIECES):
        lax.fori_loop(8 // PIECES * half, 8 // PIECES * (half + 1), last_stage, 0, unroll=8 // PIECES)

        def send_back(step, carry, half=half):
            to = lax.rem(side + 1 - step // 8, 2) * 8 + lax.rem(seat + step + 1, 8)
            back_copy(to, me, half).start()
            return carry

        lax.fori_loop(0, 15, send_back, 0)

    own_back = pltpu.make_async_copy(
        ysend_v.at[:, pl.ds(pl.multiple_of(me * 16, 16), 16), :], brecv_v.at[me], local_sem.at[1]
    )
    own_back.start()
    def cross_group(group, carry):
        spec = spec_v[group]
        sr, si = spec[:LANES], spec[LANES:]
        rr, ri = pltpu.roll(sr, HALF, 1), pltpu.roll(si, HALF, 1)
        cross = ri * sr - rr * si
        cross = jnp.where(low_lanes(LANES), cross, -cross)
        freq = jnp.concatenate([sr * rr + si * ri, cross], axis=0).astype(BF16)
        back = dot(secondt_v[group], freq).astype(BF16).reshape(16, 16, LANES)
        y_v[:, pl.ds(pl.multiple_of(group * 16, 16), 16), :] = back
        return carry

    def cross_last(pair, carry):
        both = jnp.concatenate([y_v[2 * pair], y_v[2 * pair + 1]], axis=1)
        both = dot(firstt_v[...], both)
        grad = jnp.where(low_lanes(256), both[:, :LANES], both[:, LANES:]) * scale
        fsend_v[pair] = grad.astype(BF16)
        return carry

    lax.fori_loop(0, GROUPS, cross_group, 0, unroll=UNROLL)
    lax.fori_loop(0, 8, cross_last, 0)
    row_y, low_x = dpi // 2, lax.rem(dpi, 2)

    def filter_copy(to, source):
        return pltpu.make_async_remote_copy(
            src_ref=fsend_v.at[:, pl.ds(pl.multiple_of(to * 64, 64), 64), :], dst_ref=frecv_v.at[source],
            send_sem=f_ss.at[0], recv_sem=f_rs.at[0], device_id={"dp": 2 * to + low_x}, device_id_type=MESH,
        )

    for step in range(1, 4):
        filter_copy(lax.rem(row_y + step, 4), row_y).start()
    own_filter = pltpu.make_async_copy(
        fsend_v.at[:, pl.ds(pl.multiple_of(row_y * 64, 64), 64), :], frecv_v.at[row_y], local_sem.at[2]
    )
    own_filter.start()
    own_back.wait()
    own_filter.wait()
    whole_filter = pltpu.make_async_remote_copy(
        src_ref=fsend_v.at[:, pl.ds(0, 192), :], dst_ref=frecv_v.at[pl.ds(0, 3)],
        send_sem=f_ss.at[0], recv_sem=f_rs.at[0], device_id={"dp": dpi}, device_id_type=MESH,
    )
    half_filter = pltpu.make_async_remote_copy(
        src_ref=hsend_v, dst_ref=hrecv_v, send_sem=h_ss.at[0], recv_sem=h_rs.at[0],
        device_id={"dp": dpi + 1 - 2 * low_x}, device_id_type=MESH,
    )

    def filter_sum(pair, start):
        rows = pl.ds(pl.multiple_of(start, 32), 32)
        value = frecv_v[0, pair, rows, :].astype(F32)
        for at in range(1, 4):
            value = value + frecv_v[at, pair, rows, :].astype(F32)
        return value

    def filter_half(pair, carry):
        hsend_v[pair] = filter_sum(pair, 32 - 32 * low_x).astype(BF16)
        return carry

    def sum_copy(to, source):
        return pltpu.make_async_remote_copy(
            src_ref=asend_v.at[to], dst_ref=arecv_v.at[source], send_sem=s_ss.at[0], recv_sem=s_rs.at[0],
            device_id={"ctx": side * 8 + to}, device_id_type=MESH,
        )

    def partial(x):
        return jnp.sum(x.reshape(CHUNK // 8, 8, LANES), axis=0)

    def down(x):
        return jnp.sum(x, axis=0, keepdims=True)

    def ready_tile(tile, carry):
        cols = pl.ds(pl.multiple_of(tile * LANES, LANES), LANES)
        gain = skip_v[:, cols]
        total = jnp.zeros((8, LANES), F32)
        for top in range(0, 256, CHUNK):
            rows = pl.ds(top, CHUNK)
            queries, keys, values = (mix_v[part, rows, cols] for part in range(3))
            cot = cot_v[rows, cols].astype(F32)
            product = (keys * values).astype(BF16).astype(F32)
            grad = (cot * queries).astype(BF16).astype(F32)
            ready_v[0, rows, cols] = gain * product
            ready_v[1, rows, cols] = gain * grad
            ready_v[2, rows, cols] = cot
            total = total + partial(grad * product)
            for part in range(3):
                cut = pl.ds(pl.multiple_of(tile * LANES + part * 1024, LANES), LANES)
                one, two, _ = earlier(cut, top, rim_v[:, cut].astype(F32)[8:16] * keep)
                xs_v[0, rows, cut] = one
                xs_v[1, rows, cut] = two
        asend_v[tile, 9:10] = down(total)
        return carry

    lax.fori_loop(0, 8, ready_tile, 0)
    def grad_tile(step, carry):
        tile = lax.rem(side * 4 + step, 8)
        cols = pl.ds(pl.multiple_of(tile * LANES, LANES), LANES)
        for core in range(2):

            @pl.when(2 * tile + core != me)
            def _():
                whole_back(2 * tile + core).wait_recv()

        pair = jnp.concatenate(
            [brecv_v[2 * tile].reshape(256, LANES), brecv_v[2 * tile + 1].reshape(256, LANES)], axis=1
        )
        pair_v[...] = dot(unperm_v[...], pair)
        totals = [jnp.zeros((8, LANES), F32)] * 9
        low = low_lanes(CHUNK)
        for top in range(0, 256, CHUNK):
            rows = pl.ds(top, CHUNK)
            even, odd = pair_v[rows, :LANES], pair_v[rows, LANES:]
            gated = jnp.where(low, even, pltpu.roll(odd, HALF, 1)) + ready_v[0, rows, cols]
            product_grad = jnp.where(low, pltpu.roll(even, HALF, 1), odd) + ready_v[1, rows, cols]
            queries, keys, values = (mix_v[part, rows, cols] for part in range(3))
            out_v[rows, cols] = (queries * gated).astype(BF16)
            grads = (ready_v[2, rows, cols] * gated, product_grad * values, product_grad * keys)
            for part, mixed_grad in enumerate(grads):
                cut = pl.ds(pl.multiple_of(tile * LANES + part * 1024, LANES), LANES)
                rounded = mixed_grad.astype(BF16)
                mg_v[rows, cut] = rounded
                mg = rounded.astype(F32)
                if top == 0:
                    rsend_v[tile, 2 * part : 2 * part + 2] = mg[:2]
                lagged = (proj_v[rows, cut].astype(F32), xs_v[0, rows, cut], xs_v[1, rows, cut])
                for tap in range(3):
                    totals[3 * part + tap] = totals[3 * part + tap] + partial(mg * lagged[tap])
        for at in range(9):
            asend_v[tile, at : at + 1] = down(totals[at])

        @pl.when(tile != seat)
        def _():
            sum_copy(tile, seat).start()

        return carry

    rsend_v[...] = jnp.zeros_like(rsend_v)
    lax.fori_loop(0, 8, grad_tile, 0, unroll=2)
    rims = pltpu.make_async_remote_copy(
        src_ref=rsend_v, dst_ref=rrecv_v, send_sem=r_ss.at[0], recv_sem=r_rs.at[0],
        device_id={"ctx": prv}, device_id_type=MESH,
    )
    arecv_v[seat] = asend_v[seat]
    whole_sums = pltpu.make_async_remote_copy(
        src_ref=asend_v.at[pl.ds(0, 7)], dst_ref=arecv_v.at[pl.ds(0, 7)],
        send_sem=s_ss.at[0], recv_sem=s_rs.at[0], device_id={"ctx": nxt}, device_id_type=MESH,
    )
    whole_sums.wait_recv()
    total = arecv_v[0]
    for at in range(1, 8):
        total = total + arecv_v[at]
    dsend_v[0] = total
    drecv_v[line] = total

    def part_copy(to, source):
        return pltpu.make_async_remote_copy(
            src_ref=dsend_v.at[0], dst_ref=drecv_v.at[source], send_sem=d_ss.at[0], recv_sem=d_rs.at[0],
            device_id=line_id(to), device_id_type=MESH,
        )

    def all_copy(to, source):
        return pltpu.make_async_remote_copy(
            src_ref=gsend_v.at[0], dst_ref=grecv_v.at[source], send_sem=g_ss.at[0], recv_sem=g_rs.at[0],
            device_id={"ctx": side * 8 + to}, device_id_type=MESH,
        )

    for step in range(1, 16):
        part_copy(lax.rem(line + step, 16), line).start()

    rims.start()
    whole_filter.wait_recv()
    lax.fori_loop(0, 8, filter_half, 0)
    half_filter.start()

    keep_back = jnp.where(me == 15, 0.0, 1.0).astype(F32)

    def last_tile(tile, carry):
        for part in range(3):
            cut = pl.ds(pl.multiple_of(tile * LANES + part * 1024, LANES), LANES)
            rim = pltpu.roll(rrecv_v[tile], 8 - 2 * part, 0) if part else rrecv_v[tile]
            rim = rim * keep_back
            w = short_v[:, cut]
            for top in range(0, 256, CHUNK):
                mg = mg_v[pl.ds(top, CHUNK), cut].astype(F32)
                after = mg_v[pl.ds(top + CHUNK, 16), cut].astype(F32)[:8] if top + CHUNK < 256 else rim
                value = w[0:1] * mg + w[1:2] * advanced(mg, after, 1) + w[2:3] * advanced(mg, after, 2)
                pg_v[pl.ds(top, CHUNK), cut] = value.astype(BF16)
        return carry


    whole_parts = pltpu.make_async_remote_copy(
        src_ref=dsend_v.at[pl.ds(0, 15)], dst_ref=drecv_v.at[pl.ds(0, 15)],
        send_sem=d_ss.at[0], recv_sem=d_rs.at[0], device_id={"ctx": nxt}, device_id_type=MESH,
    )
    whole_parts.wait_recv()
    total = drecv_v[0]
    for at in range(1, 16):
        total = total + drecv_v[at]
    total = total * scale
    gsend_v[0] = total
    grecv_v[seat] = total
    for step in range(1, 8):
        all_copy(lax.rem(seat + step, 8), seat).start()

    rims.wait_recv()
    lax.fori_loop(0, 8, last_tile, 0)
    half_filter.wait_recv()
    for pair in range(8):
        value = filter_sum(pair, 32 * low_x) + hrecv_v[pair].astype(F32)
        wide_v[pl.ds(2 * pair, 32, 16), :] = value
        wide_v[pl.ds(2 * pair + 1, 32, 16), :] = pltpu.roll(value, HALF, 1)
    fg_v[...] = jnp.transpose(wide_v[...])[:HALF]
    whole_forward.wait_send()
    whole_back(me).wait_send()
    whole_filter.wait_send()
    half_filter.wait_send()
    rims.wait_send()
    whole_sums.wait_send()
    whole_parts.wait_send()
    whole_all = pltpu.make_async_remote_copy(
        src_ref=gsend_v.at[pl.ds(0, 7)], dst_ref=grecv_v.at[pl.ds(0, 7)],
        send_sem=g_ss.at[0], recv_sem=g_rs.at[0], device_id={"ctx": nxt}, device_id_type=MESH,
    )
    whole_all.wait_recv()
    whole_all.wait_send()


def result_kernel(out_v, pg_v, sums_v, fg_v, out_r, pg_r, sg_r, skg_r, fg_r, sg_v, skg_v, sem):
    copies = [
        pltpu.make_async_copy(src, dst, sem.at[at])
        for at, (src, dst) in enumerate([(pg_v, pg_r), (out_v, out_r), (fg_v, fg_r), (sg_v, sg_r), (skg_v, skg_r)])
    ]
    for copy in copies[:3]:
        copy.start()
    for tile in range(8):
        for at in range(9):
            part, tap = at // 3, at % 3
            left = part * 1024 + tile * LANES
            sg_v[tap : tap + 1, left : left + LANES] = sums_v[tile, at : at + 1]
        skg_v[:, tile * LANES : tile * LANES + LANES] = sums_v[tile, 9:10]
    for copy in copies[3:]:
        copy.start()
    for copy in copies:
        copy.wait()


def shards(proj, short_w, filt, skip_gain, cotangent):
    width = skip_gain.shape[0]
    scale = 1.0 / math.sqrt(proj.shape[0] * lax.axis_size("dp") * lax.axis_size("ctx"))
    whole = pl.BlockSpec(memory_space=pl.ANY)
    inside = pl.BlockSpec(memory_space=pltpu.VMEM)
    dma = pltpu.SemaphoreType.DMA
    outs = pl.pallas_call(
        functools.partial(kernel, scale),
        out_shape=[
            pltpu.VMEM((256, 1024), BF16),
            pltpu.VMEM((256, 3072), BF16),
            pltpu.VMEM((8, 16, LANES), F32),
            pltpu.VMEM((HALF, 512), F32),
        ],
        in_specs=[whole] * 11,
        out_specs=[inside] * 4,
        scratch_shapes=[
            pltpu.VMEM((256, 3072), BF16),
            pltpu.VMEM((256, 1024), BF16),
            pltpu.VMEM((HALF, 4096), F32),
            pltpu.VMEM((3, 3072), F32),
            pltpu.VMEM((1, 1024), F32),
            pltpu.VMEM((256, 256), BF16),
            pltpu.VMEM((256, 256), BF16),
            pltpu.VMEM((2 * HI, HI), BF16),
            pltpu.VMEM((GROUPS, 256, 256), BF16),
            pltpu.VMEM((HI, 2 * HI), BF16),
            pltpu.VMEM((GROUPS, 256, 256), BF16),
            pltpu.VMEM((16, 3072), BF16),
            pltpu.VMEM((3, 256, 1024), F32),
            pltpu.VMEM((16, 16, 16, LANES), BF16),
            pltpu.VMEM((LO, HI, LANES), BF16),
            pltpu.VMEM((LO, HI, LANES), BF16),
            pltpu.VMEM((LO, 2 * HI, LANES), BF16),
            pltpu.VMEM((GROUPS, 256, LANES), F32),
            pltpu.VMEM((GROUPS, 256, LANES), F32),
            pltpu.VMEM((LO, 2 * HI, LANES), BF16),
            pltpu.VMEM((LO, HI, LANES), BF16),
            pltpu.VMEM((16, LO, 16, LANES), BF16),
            pltpu.VMEM((8, HI, LANES), BF16),
            pltpu.VMEM((4, 8, 64, LANES), BF16),
            pltpu.VMEM((8, 32, LANES), BF16),
            pltpu.VMEM((8, 32, LANES), BF16),
            pltpu.VMEM((2, 256, 3072), F32),
            pltpu.VMEM((3, 256, 1024), F32),
            pltpu.VMEM((256, 3072), BF16),
            pltpu.VMEM((256, 2 * LANES), BF16),
            pltpu.VMEM((256, 2 * LANES), F32),
            pltpu.VMEM((8, 8, LANES), F32),
            pltpu.VMEM((8, 8, LANES), F32),
            pltpu.VMEM((8, 16, LANES), F32),
            pltpu.VMEM((8, 16, LANES), F32),
            pltpu.VMEM((16, 16, LANES), F32),
            pltpu.VMEM((16, 16, LANES), F32),
            pltpu.VMEM((8, 16, LANES), F32),
            pltpu.VMEM((512, LANES), F32),
            dma((9,)), dma((4, 2)),
            dma((1,)), dma((1,)), dma((1,)), dma((1,)), dma((1,)), dma((16,)), dma((1,)), dma((1,)),
            dma((1,)), dma((1,)), dma((1,)), dma((1,)), dma((1,)), dma((1,)), dma((1,)), dma((1,)),
            dma((1,)), dma((1,)), dma((3,)),
        ],
        compiler_params=pltpu.CompilerParams(
            collective_id=0, has_side_effects=True, vmem_limit_bytes=56 * 1024 * 1024
        ),
    )(proj, cotangent, filt.T, short_w, skip_gain.reshape(1, width), *tables())
    outs = [pltpu.with_memory_space_constraint(value, pltpu.VMEM) for value in outs]
    outputs, proj_grad, short_grad, skip_grad, filt_grad = pl.pallas_call(
        result_kernel,
        out_shape=[
            jax.ShapeDtypeStruct((256, 1024), BF16),
            jax.ShapeDtypeStruct((256, 3072), BF16),
            jax.ShapeDtypeStruct((3, 3072), F32),
            jax.ShapeDtypeStruct((1, 1024), F32),
            jax.ShapeDtypeStruct((HALF, 512), F32),
        ],
        in_specs=[inside] * 4,
        out_specs=[whole] * 5,
        scratch_shapes=[pltpu.VMEM((3, 3072), F32), pltpu.VMEM((1, 1024), F32), dma((5,))],
    )(*outs)
    return (outputs, proj_grad, short_grad, skip_grad.reshape(width), filt_grad.T)


def solution(mesh):
    placed = (P(("dp", "ctx"), None), P(), P(None, "ctx"), P(), P(("dp", "ctx"), None))
    return jax.shard_map(
        shards,
        mesh=mesh,
        in_specs=placed,
        out_specs=(P(("dp", "ctx"), None), P(("dp", "ctx"), None), P(), P(), P("dp", "ctx")),
        check_vma=False,
    )
```
